256 devices in a mesh: pipe: 8 (over z_hi, x), dp: 4 (over y), tensor: 8 (over z_lo, core).
Axes of the slice: x: 4, y: 4, z: 8 (z_hi: 2, z_lo: 4; z = z_hi * 4 + z_lo), core: 2. Of those that a mesh axis runs over, the one named last changes fastest.
Arguments:
- enc_states: bfloat16 [4, 128, 8192], P('dp', None, ('pipe', 'tensor')), may hold values from -6 to 6
- enc_len: int32 [4], P('dp'), may hold values from 64 to 128
- queries: bfloat16 [8, 4, 256, 8192], P('pipe', 'dp', None, 'tensor'), may hold values from -500 to 500
- kv_weight: bfloat16 [8, 8192, 2, 8192], P('pipe', 'dp', None, 'tensor'), may hold values from -0.0625 to 0.0625
- ctx_grad: bfloat16 [8, 4, 256, 8192], P('pipe', 'dp', None, 'tensor'), may hold values from -24 to 24
Outputs:
- context: bfloat16 [8, 4, 256, 8192], P('pipe', 'dp', None, 'tensor')
- enc_grad: float32 [4, 128, 8192], P('dp', None, ('pipe', 'tensor'))
The draws below stay inside these ranges and needn't reach their ends.
All inputs are finite; a program needn't handle non-finite values.
Results may differ from the reference program's by a relative error of at most 0.014.
Values may be sent and summed in bfloat16 or wider, within the bound.
A program may use at most 192 MiB of HBM per device.

```python
import math
import jax
import jax.numpy as jnp
from jax import lax

D = 8192
HEAD_DIM = 128
ENC_LEN = 128
DEC_LEN = 256
HEADS = 64
SECTIONS = 8
REPLICAS = 4


def draw_queries(key, part):
    key = jax.random.fold_in(key, 7)
    full_shape = (SECTIONS, REPLICAS, DEC_LEN, HEADS * HEAD_DIM)
    normal_part = jnp.clip(jax.random.normal(jax.random.fold_in(key, 1), full_shape, jnp.float32), -5.0, 5.0)
    return normal_part.astype(jnp.bfloat16)


def set_ends(result, rng, low, high):
    place = [jax.random.randint(jax.random.fold_in(rng, axis), (), 0, length) for axis, length in enumerate(result.shape)]
    longest = result.shape.index(max(result.shape))
    next_to = place[:longest] + [(place[longest] + 1) % result.shape[longest]] + place[longest + 1:]
    return result.at[tuple(place)].set(low).at[tuple(next_to)].set(high)


def steps_of(key, dims, cuts, low, top_value):
    def one(axis_at, parts):
        steps = jax.random.uniform(jax.random.fold_in(jax.random.fold_in(key, 6), axis_at), (parts,), jnp.float32, low / len(cuts), top_value / len(cuts))
        return jnp.repeat(jnp.exp(steps), dims[axis_at] // parts).reshape((-1,) + (1,) * (len(dims) - axis_at - 1))

    factor_of = one(*cuts[0])
    for cut in cuts[1:]:
        factor_of = factor_of * one(*cut)
    return factor_of


def centred(key, shape, scale, bound, split=(), kind=jnp.bfloat16):
    array = scale * jax.random.normal(key, shape, jnp.float32)
    if split:
        array = array * steps_of(key, shape, split, -0.22, 0.18)
    return jnp.clip(array, -bound, bound).astype(kind)


def setup_inputs(seed: int = 0) -> dict:
    keys = jax.random.split(jax.random.key(seed), 6)
    enc_states = centred(keys[0], (REPLICAS, ENC_LEN, D), 1.0, 6.0, ((0, 4), (2, 64)))
    enc_len = set_ends(jax.random.randint(keys[1], (REPLICAS,), ENC_LEN // 2, ENC_LEN + 1), jax.random.fold_in(keys[1], 1), ENC_LEN // 2, ENC_LEN).astype(jnp.int32)
    queries = draw_queries(jax.random.fold_in(keys[5], 71), 0)
    kv_weight = centred(keys[3], (SECTIONS, D, 2, HEADS * HEAD_DIM), D ** -0.5, 0.0625, ((0, 8), (1, 4), (3, 8)))
    ctx_grad = centred(keys[4], (SECTIONS, REPLICAS, DEC_LEN, HEADS * HEAD_DIM), 4.0, 24.0, ((0, 8), (1, 4), (3, 8)))
    return dict(enc_states=enc_states, enc_len=enc_len, queries=queries, kv_weight=kv_weight, ctx_grad=ctx_grad)


def attend_one(states, length, query_rows, grad_rows, flat_weight):
    head_cols = HEADS * HEAD_DIM
    factor = 1.0 / math.sqrt(HEAD_DIM)
    highest = lax.Precision.HIGHEST
    keys_values = jnp.dot(states, flat_weight, preferred_element_type=jnp.float32)
    keys_part = keys_values[:, :head_cols].reshape(ENC_LEN, HEADS, HEAD_DIM)
    values_part = keys_values[:, head_cols:].reshape(ENC_LEN, HEADS, HEAD_DIM)
    query_heads = query_rows.reshape(DEC_LEN, HEADS, HEAD_DIM).astype(jnp.float32)
    grad_heads = grad_rows.reshape(DEC_LEN, HEADS, HEAD_DIM).astype(jnp.float32)
    scores = jnp.einsum('qhd,khd->hqk', query_heads, keys_part, precision=highest) * factor
    live_keys = jnp.arange(ENC_LEN, dtype=jnp.int32) < length
    scores = jnp.where(live_keys[None, None, :], scores, -1e+30)
    top_score = lax.optimization_barrier(jnp.max(scores, axis=-1, keepdims=True))
    expd = jnp.exp(scores - top_score)
    probs_all = expd / lax.optimization_barrier(jnp.sum(expd, axis=-1, keepdims=True))
    attn_bf = probs_all.astype(jnp.bfloat16)
    context = jnp.einsum('hqk,khd->qhd', attn_bf.astype(jnp.float32), values_part, precision=highest)
    context = context.reshape(DEC_LEN, head_cols).astype(jnp.bfloat16)
    probs_grad = jnp.einsum('qhd,khd->hqk', grad_heads, values_part, precision=highest)
    row_dots = lax.optimization_barrier(jnp.sum(probs_all * probs_grad, axis=-1, keepdims=True))
    score_grad = (probs_all * (probs_grad - row_dots) * factor).astype(jnp.bfloat16)
    key_grad = jnp.einsum('hqk,qhd->khd', score_grad.astype(jnp.float32), query_heads)
    value_grad = jnp.einsum('hqk,qhd->khd', attn_bf.astype(jnp.float32), grad_heads)
    kv_grad = jnp.concatenate([key_grad.reshape(ENC_LEN, head_cols), value_grad.reshape(ENC_LEN, head_cols)], axis=1).astype(jnp.bfloat16)
    grad_term = jnp.dot(kv_grad, flat_weight.T, preferred_element_type=jnp.float32)
    return (context, grad_term)

def reference(enc_states, enc_len, queries, kv_weight, ctx_grad):

    def one_layer(grad_sum, layer_args):
        weight_layer, query_layer, grad_layer = layer_args
        flat_weight = weight_layer.reshape(D, 2 * HEADS * HEAD_DIM)
        contexts = []
        terms = []
        for replica in range(REPLICAS):
            context, grad_term = attend_one(enc_states[replica], enc_len[replica], query_layer[replica], grad_layer[replica], flat_weight)
            contexts.append(context)
            terms.append(grad_term)
        return (grad_sum + jnp.stack(terms), jnp.stack(contexts))
    start_sum = jnp.zeros((REPLICAS, ENC_LEN, D), jnp.float32)
    enc_grad, context = lax.scan(one_layer, start_sum, (kv_weight, queries, ctx_grad))
    return (context, enc_grad)
```

```python
import math

import jax
import jax.numpy as jnp
from jax import lax
from jax.experimental import pallas as pl
from jax.experimental.pallas import tpu as pltpu
from jax.sharding import PartitionSpec as P

HEAD_DIM = 128
TOK = 128
FB = 128
HEADS_HERE = 8
COLS = HEADS_HERE * HEAD_DIM
DEC = 256
ROWS = 2048
HALF = ROWS // 2
BF = jnp.bfloat16
F32 = jnp.float32
MESH = pl.DeviceIdType.MESH


def dot(a, b, dims):
    return lax.dot_general(a, b, (dims, ((), ())), preferred_element_type=F32)


def kernel(
    x_ref, len_ref, q_hbm, w_hbm, g_hbm, ctx_hbm, out_ref,
    states, w, q, g, kb, vb, kr, vr, kvg, ctx, po, ps, pr, s2, r2, tot, s3, r3, s4, r4,
    w_sem, in_sem, a1s, a1r, a2s, a2r, a3s, a3r, a4s, a4r,
    bks, bkr, bvs, bvr, cs, cr, e1s, e1r, e2s, e2r, e3s, e3r, e4s, e4r,
):
    p = lax.axis_index("pipe")
    y = lax.axis_index("dp")
    t = lax.axis_index("tensor")
    zh, x = p // 4, p % 4
    zl, core = t // 2, t % 2
    z = zh * 4 + zl

    def at(x_, y_, z_, core_):
        return ((z_ // 4) * 4 + x_, y_, (z_ % 4) * 2 + core_)

    def remote(src, dst, send, recv, dev):
        return pltpu.make_async_remote_copy(
            src_ref=src, dst_ref=dst, send_sem=send, recv_sem=recv,
            device_id=dev, device_id_type=MESH,
        )

    def lanes(index, size):
        return pl.ds(pl.multiple_of(index * size, size), size)

    zs = [at(x, y, (z + k) % 8, core) for k in range(8)]
    xs = [at((x + k) % 4, y, z, core) for k in range(4)]
    ys = [at(x, (y + k) % 4, z, core) for k in range(4)]
    sibling = at(x, y, z, 1 - core)
    hold_z = (1 - p % 2) * 4 + zl
    holder = at(y, p // 2, hold_z, core)
    owner = (2 * y + (1 - zh), x, t)

    loads = []
    for place in range(16):
        c_, z_ = place // 8, place % 8
        block = (1 - z_ // 4) * 8 + (z_ % 4) * 2 + c_
        loads.append(
            pltpu.make_async_copy(
                w_hbm.at[pl.ds(block * FB, FB)], w.at[pl.ds(place * FB, FB)], w_sem.at[place]
            )
        )
    load_q = pltpu.make_async_copy(q_hbm, q, in_sem.at[0])
    load_g = pltpu.make_async_copy(g_hbm, g, in_sem.at[1])
    for load in loads + [load_q, load_g]:
        load.start()

    barrier = pltpu.get_barrier_semaphore()
    partners = zs[1:] + xs[1:] + ys[1:] + [sibling, holder, owner]
    for dev in partners:
        pl.semaphore_signal(barrier, inc=1, device_id=dev, device_id_type=MESH)
    pl.semaphore_wait(barrier, len(partners))

    first = remote(
        x_ref, states.at[y, :, lanes(core * 8 + hold_z, FB)], a1s.at[0], a1r.at[0], holder
    )
    first.start()
    mine = states.at[x, :, lanes(core * 8 + z, FB)]
    remote(x_ref, mine, a1s.at[0], a1r.at[0], holder).wait_recv()
    along_z = [remote(mine, mine, a2s.at[k - 1], a2r.at[k - 1], zs[k]) for k in range(1, 8)]
    for copy in along_z:
        copy.start()
    for k in range(1, 8):
        theirs = states.at[x, :, lanes(core * 8 + (z + 8 - k) % 8, FB)]
        remote(theirs, theirs, a2s.at[k - 1], a2r.at[k - 1], zs[k]).wait_recv()
    row = states.at[x, :, lanes(core, HALF)]
    along_x = [remote(row, row, a3s.at[k - 1], a3r.at[k - 1], xs[k]) for k in range(1, 4)]
    for copy in along_x:
        copy.start()
    across = []
    for k in range(4):
        seq = (x + 4 - k) % 4
        row = states.at[seq, :, lanes(core, HALF)]
        if k:
            remote(row, row, a3s.at[k - 1], a3r.at[k - 1], xs[k]).wait_recv()
        across.append(remote(row, row, a4s.at[k], a4r.at[k], sibling))
        across[-1].start()
    for k in range(4):
        row = states.at[(x + 4 - k) % 4, :, lanes(1 - core, HALF)]
        remote(row, row, a4s.at[k], a4r.at[k], sibling).wait_recv()
    for load in loads:
        load.wait()

    def project(c, _):
        cols = lanes(c, 256)
        vcols = pl.ds(pl.multiple_of(COLS + c * 256, 256), 256)
        lhs = states[...].reshape(4 * TOK, ROWS)
        kb[:, :, cols] = dot(lhs, w[:, cols], ((1,), (0,))).reshape(4, TOK, 256)
        vb[:, :, cols] = dot(lhs, w[:, vcols], ((1,), (0,))).reshape(4, TOK, 256).astype(BF)
        return 0

    lax.fori_loop(0, COLS // 256, project, 0)

    key_copies, value_copies = {}, {}
    for k in (2, 1, 3):
        seq = (y + k) % 4
        key_copies[k] = remote(kb.at[seq], kr.at[k - 1], bks.at[k - 1], bkr.at[k - 1], ys[k])
        value_copies[k] = remote(vb.at[seq], vr.at[k - 1], bvs.at[k - 1], bvr.at[k - 1], ys[k])
        key_copies[k].start()
        value_copies[k].start()
    load_q.wait()
    load_g.wait()
    for k in (1, 3, 2):
        key_copies[k].wait_recv()
        value_copies[k].wait_recv()

    factor = 1.0 / math.sqrt(HEAD_DIM)
    live = lax.broadcasted_iota(jnp.int32, (TOK, DEC), 0) < len_ref[0]

    def one_head(h):
        cols = lanes(h, HEAD_DIM)
        vcols = pl.ds(pl.multiple_of(COLS + h * HEAD_DIM, HEAD_DIM), HEAD_DIM)
        keys = kb[y, :, cols] + kr[0, :, cols] + kr[1, :, cols] + kr[2, :, cols]
        values = (
            vb[y, :, cols].astype(F32) + vr[0, :, cols].astype(F32)
            + vr[1, :, cols].astype(F32) + vr[2, :, cols].astype(F32)
        )
        k1 = keys.astype(BF)
        rest = keys - k1.astype(F32)
        k2 = rest.astype(BF)
        k3 = (rest - k2.astype(F32)).astype(BF)
        v1 = values.astype(BF)
        v2 = (values - v1.astype(F32)).astype(BF)
        qh, gh = q[:, cols], g[:, cols]
        nt, nn, tn = ((1,), (1,)), ((1,), (0,)), ((0,), (0,))
        scores = (dot(k3, qh, nt) + dot(k2, qh, nt) + dot(k1, qh, nt)) * factor
        scores = jnp.where(live, scores, -1e30)
        top = jnp.max(scores, axis=0, keepdims=True)
        expd = jnp.exp(scores - top)
        probs = expd / jnp.sum(expd, axis=0, keepdims=True)
        attn = probs.astype(BF)
        ctx[:, cols] = (dot(attn, v2, tn) + dot(attn, v1, tn)).astype(BF)
        probs_grad = dot(v2, gh, nt) + dot(v1, gh, nt)
        row_dots = jnp.sum(probs * probs_grad, axis=0, keepdims=True)
        score_grad = (probs * (probs_grad - row_dots) * factor).astype(BF)
        kvg[0, :, cols] = dot(score_grad, qh, nn).astype(BF)
        kvg[0, :, vcols] = dot(attn, gh, nn).astype(BF)

    def two_heads(i, _):
        one_head(2 * i)
        one_head(2 * i + 1)
        return 0

    lax.fori_loop(0, HEADS_HERE // 2, two_heads, 0)

    save_ctx = pltpu.make_async_copy(ctx, ctx_hbm, in_sem.at[2])
    save_ctx.start()
    grad_copies = {}
    for k in (2, 1, 3):
        grad_copies[k] = remote(kvg.at[0], kvg.at[4 - k], cs.at[k - 1], cr.at[k - 1], ys[k])
        grad_copies[k].start()
    for k in (1, 3, 2):
        back = kvg.at[4 - k]
        remote(back, back, cs.at[k - 1], cr.at[k - 1], ys[k]).wait_recv()

    def terms(half, i):
        rows = pl.ds(pl.multiple_of(half * HALF + i * 256, 256), 256)
        return dot(w[rows, :], kvg[...].reshape(4 * TOK, 2 * COLS), ((1,), (1,)))

    def give(i):
        return remote(
            ps.at[:, pl.ds(i * 256, 256)], pr.at[:, pl.ds(i * 256, 256)],
            e1s.at[i], e1r.at[i], sibling,
        )

    for i in range(4):
        acc = terms(1 - core, i)
        for k in range(4):
            ps[(y + k) % 4, pl.ds(i * 256, 256), :] = acc[:, k * TOK:(k + 1) * TOK].astype(BF)
        give(i).start()
    for i in range(4):
        acc = terms(core, i)
        for k in range(4):
            po[(y + k) % 4, pl.ds(i * 256, 256), :] = acc[:, k * TOK:(k + 1) * TOK]
    for i in range(4):
        give(i).wait_recv()

    out_x = [remote(s2.at[k], r2.at[k], e2s.at[k], e2r.at[k], xs[k + 1]) for k in range(3)]
    for k in (1, 0, 2):
        seq = (x + k + 1) % 4
        s2[k] = (po[seq] + pr[seq].astype(F32)).astype(BF)
        out_x[k].start()
    tot[...] = (po[x] + pr[x].astype(F32)).reshape(8, FB, TOK)
    for k in (0, 2, 1):
        out_x[k].wait_recv()
        tot[...] += r2[k].astype(F32).reshape(8, FB, TOK)
    out_z = []
    for k in (4, 3, 5, 2, 6, 1, 7):
        s3[k - 1] = tot[(z + k) % 8].astype(BF)
        out_z.append(remote(s3.at[k - 1], r3.at[k - 1], e3s.at[k - 1], e3r.at[k - 1], zs[k]))
        out_z[-1].start()
    for copy in out_z:
        copy.wait_recv()
    total = tot[z]
    for k in range(7):
        total += r3[k].astype(F32)
    s4[...] = total.T
    last = remote(s4, r4, e4s.at[0], e4r.at[0], owner)
    last.start()
    last.wait_recv()
    out_ref[...] = r4[...]

    save_ctx.wait()
    first.wait_send()
    last.wait_send()
    for copy in along_z + along_x + across + out_x + out_z:
        copy.wait_send()
    for k in (1, 2, 3):
        key_copies[k].wait_send()
        value_copies[k].wait_send()
        grad_copies[k].wait_send()
    for i in range(4):
        give(i).wait_send()


def on_device(enc_states, enc_len, queries, kv_weight, ctx_grad):
    any_spec = pl.BlockSpec(memory_space=pl.ANY)
    vmem = pltpu.VMEM
    dma = lambda n: pltpu.SemaphoreType.DMA((n,))
    context, enc_grad = pl.pallas_call(
        kernel,
        out_shape=(
            jax.ShapeDtypeStruct((DEC, COLS), BF),
            jax.ShapeDtypeStruct((TOK, FB), F32),
        ),
        in_specs=[any_spec, pl.BlockSpec(memory_space=pltpu.SMEM)] + [any_spec] * 3,
        out_specs=(any_spec, pl.BlockSpec(memory_space=pltpu.VMEM)),
        scratch_shapes=[
            vmem((4, TOK, ROWS), BF),
            vmem((ROWS, 2 * COLS), BF),
            vmem((DEC, COLS), BF),
            vmem((DEC, COLS), BF),
            vmem((4, TOK, COLS), F32),
            vmem((4, TOK, COLS), BF),
            vmem((3, TOK, COLS), F32),
            vmem((3, TOK, COLS), BF),
            vmem((4, TOK, 2 * COLS), BF),
            vmem((DEC, COLS), BF),
            vmem((4, HALF, TOK), F32),
            vmem((4, HALF, TOK), BF),
            vmem((4, HALF, TOK), BF),
            vmem((3, HALF, TOK), BF),
            vmem((3, HALF, TOK), BF),
            vmem((8, FB, TOK), F32),
            vmem((7, FB, TOK), BF),
            vmem((7, FB, TOK), BF),
            vmem((TOK, FB), F32),
            vmem((TOK, FB), F32),
            dma(16), dma(3), dma(1), dma(1), dma(7), dma(7), dma(3), dma(3), dma(4), dma(4),
            dma(3), dma(3), dma(3), dma(3), dma(3), dma(3), dma(4), dma(4),
            dma(3), dma(3), dma(7), dma(7), dma(1), dma(1),
        ],
        compiler_params=pltpu.CompilerParams(
            collective_id=0, has_side_effects=True, vmem_limit_bytes=50 * 2**20
        ),
    )(
        enc_states[0],
        enc_len,
        queries[0, 0],
        kv_weight[0].reshape(ROWS, 2 * COLS),
        ctx_grad[0, 0],
    )
    return (context[None, None], enc_grad[None])


def solution(mesh):
    return jax.shard_map(
        on_device,
        mesh=mesh,
        in_specs=(
            P("dp", None, ("pipe", "tensor")),
            P("dp"),
            P("pipe", "dp", None, "tensor"),
            P("pipe", "dp", None, "tensor"),
            P("pipe", "dp", None, "tensor"),
        ),
        out_specs=(P("pipe", "dp", None, "tensor"), P("dp", None, ("pipe", "tensor"))),
        check_vma=False,
    )
```

```python
import math

import jax
import jax.numpy as jnp
from jax import lax
from jax.experimental import pallas as pl
from jax.experimental.pallas import tpu as pltpu
from jax.sharding import PartitionSpec as P

HEAD_DIM = 128
TOK = 128
FB = 128
HEADS_HERE = 8
GROUPS = 4
COLS = HEADS_HERE * HEAD_DIM
DEC = 256
ROWS = 2048
HALF = ROWS // 2
BF = jnp.bfloat16
F32 = jnp.float32
MESH = pl.DeviceIdType.MESH


def dot(a, b, dims):
    return lax.dot_general(a, b, (dims, ((), ())), preferred_element_type=F32)


def kernel(
    x_ref, len_ref, q_hbm, w_hbm, g_hbm, ctx_hbm, out_ref,
    states, wv, w, q, g, kb, vb, mk, mv, fk, fv, kr, vr, kvg, ctx,
    po, ps, pr, s2, r2, tot, s3, r3, mine, s4, r4,
    in_sem, a1s, a1r, a2s, a2r, a3s, a3r, a4s, a4r,
    bs, br, cs, cr, e1s, e1r, e2s, e2r, e3s, e3r, e4s, e4r,
):
    p = lax.axis_index("pipe")
    y = lax.axis_index("dp")
    t = lax.axis_index("tensor")
    zh, x = p // 4, p % 4
    zl, core = t // 2, t % 2
    z = zh * 4 + zl

    def at(x_, y_, z_, core_):
        return ((z_ // 4) * 4 + x_, y_, (z_ % 4) * 2 + core_)

    sent = []

    def remote(src, dst, send, recv, dev):
        return pltpu.make_async_remote_copy(
            src_ref=src, dst_ref=dst, send_sem=send, recv_sem=recv,
            device_id=dev, device_id_type=MESH,
        )

    def post(src, dst, send, recv, dev):
        copy = remote(src, dst, send, recv, dev)
        copy.start()
        sent.append(copy)

    def arrived(dst, send, recv):
        remote(dst, dst, send, recv, sibling).wait_recv()

    def part(index, size):
        return pl.ds(pl.multiple_of(index * size, size), size)

    zs = [at(x, y, (z + k) % 8, core) for k in range(8)]
    xs = [at((x + k) % 4, y, z, core) for k in range(4)]
    right, left = at(x, (y + 1) % 4, z, core), at(x, (y + 3) % 4, z, core)
    sibling = at(x, y, z, 1 - core)
    hold_x, hold_z = zl, 2 * y + 1 - p % 2
    holder = at(hold_x, p // 2, hold_z, core)
    owner = (2 * y + 1 - z % 2, z // 2, x * 2 + core)

    load_w = pltpu.make_async_copy(w_hbm, wv, in_sem.at[0])
    load_q = pltpu.make_async_copy(q_hbm, q, in_sem.at[1])
    load_g = pltpu.make_async_copy(g_hbm, g, in_sem.at[2])
    for load in (load_w, load_q, load_g):
        load.start()

    barrier = pltpu.get_barrier_semaphore()
    partners = zs[1:] + xs[1:] + [right, left, sibling, holder, owner]
    for dev in partners:
        pl.semaphore_signal(barrier, inc=1, device_id=dev, device_id_type=MESH)
    pl.semaphore_wait(barrier, len(partners))

    post(
        x_ref, states.at[y, :, part(core * 8 + hold_x * 2 + hold_z % 2, FB)],
        a1s.at[0], a1r.at[0], holder,
    )

    load_w.wait()

    def lay(i, _):
        block, sub = i // 4, i % 4
        place = (block % 2) * 8 + (block % 8 // 2) * 2 + 1 - block // 8
        rows = part(place * 4 + sub, 32)
        flat = wv[part(i, 32)].reshape(32, 2 * COLS)
        for n in range(GROUPS):
            w[rows, n * 512:n * 512 + 256] = flat[:, n * 256:(n + 1) * 256]
            w[rows, n * 512 + 256:(n + 1) * 512] = flat[:, COLS + n * 256:COLS + (n + 1) * 256]
        return 0

    lax.fori_loop(0, ROWS // 32, lay, 0)
    own = states.at[z // 2, :, part(core * 8 + x * 2 + z % 2, FB)]
    arrived(own, a1s.at[0], a1r.at[0])
    for k in (1, 7, 2, 6, 3, 5, 4):
        post(own, own, a2s.at[k - 1], a2r.at[k - 1], zs[k])
    order = (0, 1, 3, 2)
    for n in order:
        seq = (z // 2 + n) % 4
        for b in range(2):
            other = 2 * seq + b if n else z + 1 - 2 * (z % 2)
            if n or b:
                block = states.at[seq, :, part(core * 8 + x * 2 + other % 2, FB)]
                k = (z + 8 - other) % 8 - 1
                arrived(block, a2s.at[k], a2r.at[k])
        pair = states.at[seq, :, part(core * 4 + x, 2 * FB)]
        for k in (2, 1, 3):
            post(pair, pair, a3s.at[k - 1, n], a3r.at[k - 1, n], xs[k])
    for n in order:
        seq = (z // 2 + n) % 4
        for k in (1, 3, 2):
            pair = states.at[seq, :, part(core * 4 + (x + 4 - k) % 4, 2 * FB)]
            arrived(pair, a3s.at[k - 1, n], a3r.at[k - 1, n])
        half = states.at[seq, :, part(core, HALF)]
        post(half, half, a4s.at[n], a4r.at[n], sibling)
    for n in order:
        half = states.at[(z // 2 + n) % 4, :, part(1 - core, HALF)]
        arrived(half, a4s.at[n], a4r.at[n])
    plus, minus, far = (y + 1) % 4, (y + 3) % 4, (y + 2) % 4

    def project(n):
        acc = dot(
            states[...].reshape(4 * TOK, ROWS), w[:, n * 512:(n + 1) * 512], ((1,), (0,))
        ).reshape(4, TOK, 512)
        for h in range(2):
            kb[n, :, h] = acc[:, :, h * 128:(h + 1) * 128]
            vb[n, :, h] = acc[:, :, 256 + h * 128:256 + (h + 1) * 128].astype(BF)
        for i, (buf, mid, last) in enumerate(((kb, mk, kr), (vb, mv, vr))):
            post(buf.at[n, far, 0], mid.at[n, 0], bs.at[n, i], br.at[n, i], right)
            post(buf.at[n, far, 1], mid.at[n, 1], bs.at[n, 2 + i], br.at[n, 2 + i], left)
            post(buf.at[n, plus, 1], last.at[n, 0, 1], bs.at[n, 4 + i], br.at[n, 4 + i], right)
            post(buf.at[n, minus, 0], last.at[n, 1, 0], bs.at[n, 6 + i], br.at[n, 6 + i], left)

    def merge(n):
        for h, (seq, dev) in enumerate(((plus, right), (minus, left))):
            arrived(mk.at[n, h], bs.at[n, 2 * h], br.at[n, 2 * h])
            fk[n, h] = mk[n, h] + kb[n, seq, h]
            post(fk.at[n, h], kr.at[n, h, h], bs.at[n, 8 + 2 * h], br.at[n, 8 + 2 * h], dev)
            arrived(mv.at[n, h], bs.at[n, 2 * h + 1], br.at[n, 2 * h + 1])
            fv[n, h] = (mv[n, h].astype(F32) + vb[n, seq, h].astype(F32)).astype(BF)
            post(fv.at[n, h], vr.at[n, h, h], bs.at[n, 9 + 2 * h], br.at[n, 9 + 2 * h], dev)

    factor = 1.0 / math.sqrt(HEAD_DIM)

    def one_head(n, h):
        live = lax.broadcasted_iota(jnp.int32, (TOK, DEC), 0) < len_ref[0]
        cols = slice((2 * n + h) * HEAD_DIM, (2 * n + h + 1) * HEAD_DIM)
        keys = kb[n, y, h] + kr[n, 0, h] + kr[n, 1, h]
        values = vb[n, y, h].astype(F32) + vr[n, 0, h].astype(F32) + vr[n, 1, h].astype(F32)
        k1 = keys.astype(BF)
        rest = keys - k1.astype(F32)
        k2 = rest.astype(BF)
        k3 = (rest - k2.astype(F32)).astype(BF)
        v1 = values.astype(BF)
        v2 = (values - v1.astype(F32)).astype(BF)
        qh, gh = q[:, cols], g[:, cols]
        nt, nn, tn = ((1,), (1,)), ((1,), (0,)), ((0,), (0,))
        scores = (dot(k3, qh, nt) + dot(k2, qh, nt) + dot(k1, qh, nt)) * factor
        scores = jnp.where(live, scores, -1e30)
        top = jnp.max(scores, axis=0, keepdims=True)
        expd = jnp.exp(scores - top)
        probs = expd / jnp.sum(expd, axis=0, keepdims=True)
        attn = probs.astype(BF)
        ctx[:, cols] = (dot(attn, v2, tn) + dot(attn, v1, tn)).astype(BF)
        probs_grad = dot(v2, gh, nt) + dot(v1, gh, nt)
        row_dots = jnp.sum(probs * probs_grad, axis=0, keepdims=True)
        score_grad = (probs * (probs_grad - row_dots) * factor).astype(BF)
        lanes = slice(h * HEAD_DIM, (h + 1) * HEAD_DIM)
        kvg[n, 0, 0, :, lanes] = dot(score_grad, qh, nn).astype(BF)
        kvg[n, 0, 1, :, lanes] = dot(attn, gh, nn).astype(BF)

    def attend(n):
        for i, last in enumerate((kr, vr)):
            arrived(last.at[n, 0, 1], bs.at[n, 4 + i], br.at[n, 4 + i])
            arrived(last.at[n, 1, 0], bs.at[n, 6 + i], br.at[n, 6 + i])
            for h in range(2):
                c = 8 + 2 * h + i
                arrived(last.at[n, h, h], bs.at[n, c], br.at[n, c])
        for h in range(2):
            one_head(n, h)
        post(kvg.at[n, 0], kvg.at[n, 3], cs.at[n, 0], cr.at[n, 0], right)
        post(kvg.at[n, 0], kvg.at[n, 1], cs.at[n, 1], cr.at[n, 1], left)

    def pass_on(n):
        arrived(kvg.at[n, 3], cs.at[n, 0], cr.at[n, 0])
        post(kvg.at[n, 3, 0], kvg.at[n, 2, 0], cs.at[n, 2], cr.at[n, 2], right)
        arrived(kvg.at[n, 1], cs.at[n, 1], cr.at[n, 1])
        post(kvg.at[n, 1, 1], kvg.at[n, 2, 1], cs.at[n, 3], cr.at[n, 3], left)

    def far_here(n):
        for h in range(2):
            arrived(kvg.at[n, 2, h], cs.at[n, 2 + h], cr.at[n, 2 + h])

    def early_terms(i, _):
        rows = part(i, 256)
        acc = jnp.zeros((256, 4 * TOK), F32)
        for n in range(2):
            for h in range(2):
                c = (2 * n + h) * 256
                acc += dot(w[rows, c:c + 256], kvg[n, :, h].reshape(4 * TOK, 256), ((1,), (1,)))
        for j in range(4):
            po[j, rows, :] = acc[:, j * TOK:(j + 1) * TOK]
        return 0

    def late_terms(half, j):
        rows = part(half, HALF)
        acc = po[j, rows, :]
        for n in range(2, GROUPS):
            for h in range(2):
                c = (2 * n + h) * 256
                acc += dot(w[rows, c:c + 256], kvg[n, j, h], ((1,), (1,)))
        return acc

    project(0)
    project(1)
    merge(0)
    project(2)
    merge(1)
    project(3)
    load_q.wait()
    load_g.wait()
    attend(0)
    merge(2)
    attend(1)
    merge(3)
    pass_on(0)
    attend(2)
    pass_on(1)
    attend(3)
    save_ctx = pltpu.make_async_copy(ctx, ctx_hbm, in_sem.at[3])
    save_ctx.start()
    pass_on(2)
    far_here(0)
    far_here(1)
    lax.fori_loop(0, ROWS // 256, early_terms, 0)

    def over_cores(j):
        ps[j] = late_terms(1 - core, j).astype(BF)
        post(ps.at[j], pr.at[j], e1s.at[j], e1r.at[j], sibling)
        po[j, part(core, HALF), :] = late_terms(core, j)

    def over_x(j):
        arrived(pr.at[j], e1s.at[j], e1r.at[j])
        both = po[j, part(core, HALF), :] + pr[j].astype(F32)
        po[j, part(core, HALF), :] = both
        s2[j] = both.astype(BF)
        for k in (2, 1, 3):
            post(
                s2.at[j, part((x + k) % 4, 2 * FB)], r2.at[k - 1, j],
                e2s.at[k - 1, j], e2r.at[k - 1, j], xs[k],
            )

    def to_z(j, b):
        to = 2 * ((y + j) % 4) + b
        k = (z + 8 - to) % 8 - 1
        return to != z, remote(
            s3.at[j, b], r3.at[jnp.maximum(k, 0)], e3s.at[2 * j + b],
            e3r.at[jnp.maximum(k, 0)], at(x, y, to, core),
        )

    def over_z(j):
        total = po[j, part(core * 4 + x, 2 * FB), :]
        for k in (1, 3, 2):
            arrived(r2.at[k - 1, j], e2s.at[k - 1, j], e2r.at[k - 1, j])
            total += r2[k - 1, j].astype(F32)
        tot[j] = total.reshape(2, FB, TOK)
        s3[j] = total.reshape(2, FB, TOK).astype(BF)
        for b in range(2):
            away, copy = to_z(j, b)

            @pl.when(away)
            def _():
                copy.start()

            @pl.when(jnp.logical_not(away))
            def _():
                mine[...] = tot[j, b]

    over_cores(0)
    pass_on(3)
    over_cores(3)
    over_x(0)
    over_cores(1)
    over_x(3)
    over_z(0)
    far_here(2)
    far_here(3)
    over_cores(2)
    over_x(1)
    over_z(3)
    over_x(2)
    over_z(1)
    over_z(2)
    total = mine[...]
    for k in range(7):
        arrived(r3.at[k], e3s.at[k], e3r.at[k])
        total += r3[k].astype(F32)
    s4[...] = total.T
    post(s4, r4, e4s.at[0], e4r.at[0], owner)
    arrived(r4, e4s.at[0], e4r.at[0])
    out_ref[...] = r4[...]

    save_ctx.wait()
    for copy in sent:
        copy.wait_send()
    for j in range(4):
        for b in range(2):
            away, copy = to_z(j, b)

            @pl.when(away)
            def _():
                copy.wait_send()


def on_device(enc_states, enc_len, queries, kv_weight, ctx_grad):
    any_spec = pl.BlockSpec(memory_space=pl.ANY)
    vmem = pltpu.VMEM
    dma = lambda *n: pltpu.SemaphoreType.DMA(n)
    context, enc_grad = pl.pallas_call(
        kernel,
        out_shape=(
            jax.ShapeDtypeStruct((DEC, COLS), BF),
            jax.ShapeDtypeStruct((TOK, FB), F32),
        ),
        in_specs=[any_spec, pl.BlockSpec(memory_space=pltpu.SMEM)] + [any_spec] * 3,
        out_specs=(any_spec, pl.BlockSpec(memory_space=pltpu.VMEM)),
        scratch_shapes=[
            vmem((4, TOK, ROWS), BF),
            vmem((ROWS, 2, COLS), BF),
            vmem((ROWS, 2 * COLS), BF),
            vmem((DEC, COLS), BF),
            vmem((DEC, COLS), BF),
            vmem((GROUPS, 4, 2, TOK, HEAD_DIM), F32),
            vmem((GROUPS, 4, 2, TOK, HEAD_DIM), BF),
            vmem((GROUPS, 2, TOK, HEAD_DIM), F32),
            vmem((GROUPS, 2, TOK, HEAD_DIM), BF),
            vmem((GROUPS, 2, TOK, HEAD_DIM), F32),
            vmem((GROUPS, 2, TOK, HEAD_DIM), BF),
            vmem((GROUPS, 2, 2, TOK, HEAD_DIM), F32),
            vmem((GROUPS, 2, 2, TOK, HEAD_DIM), BF),
            vmem((GROUPS, 4, 2, TOK, 2 * HEAD_DIM), BF),
            vmem((DEC, COLS), BF),
            vmem((4, ROWS, TOK), F32),
            vmem((4, HALF, TOK), BF),
            vmem((4, HALF, TOK), BF),
            vmem((4, HALF, TOK), BF),
            vmem((3, 4, 2 * FB, TOK), BF),
            vmem((4, 2, FB, TOK), F32),
            vmem((4, 2, FB, TOK), BF),
            vmem((7, FB, TOK), BF),
            vmem((FB, TOK), F32),
            vmem((TOK, FB), F32),
            vmem((TOK, FB), F32),
            dma(4), dma(1), dma(1), dma(7), dma(7), dma(3, 4), dma(3, 4), dma(4), dma(4),
            dma(GROUPS, 12), dma(GROUPS, 12), dma(GROUPS, 4), dma(GROUPS, 4), dma(4), dma(4),
            dma(3, 4), dma(3, 4), dma(8), dma(7), dma(1), dma(1),
        ],
        compiler_params=pltpu.CompilerParams(
            collective_id=0, has_side_effects=True, vmem_limit_bytes=56 * 2**20
        ),
    )(
        enc_states[0],
        enc_len,
        queries[0, 0],
        kv_weight[0],
        ctx_grad[0, 0],
    )
    return (context[None, None], enc_grad[None])


def solution(mesh):
    return jax.shard_map(
        on_device,
        mesh=mesh,
        in_specs=(
            P("dp", None, ("pipe", "tensor")),
            P("dp"),
            P("pipe", "dp", None, "tensor"),
            P("pipe", "dp", None, "tensor"),
            P("pipe", "dp", None, "tensor"),
        ),
        out_specs=(P("pipe", "dp", None, "tensor"), P("dp", None, ("pipe", "tensor"))),
        check_vma=False,
    )
```

```python
import math

import jax
import jax.numpy as jnp
from jax import lax
from jax.experimental import pallas as pl
from jax.experimental.pallas import tpu as pltpu
from jax.sharding import PartitionSpec as P

HEAD_DIM = 128
TOK = 128
FB = 128
HEADS_HERE = 8
GROUPS = 4
COLS = HEADS_HERE * HEAD_DIM
DEC = 256
ROWS = 2048
HALF = ROWS // 2
BF = jnp.bfloat16
F32 = jnp.float32
MESH = pl.DeviceIdType.MESH


def dot(a, b, dims):
    return lax.dot_general(a, b, (dims, ((), ())), preferred_element_type=F32)


def kernel(
    x_ref, len_ref, q_hbm, w_hbm, g_hbm, ctx_hbm, out_ref,
    states, wv, w, q, g, kb, vb, mk, mv, fk, fv, kr, vr, kvg, ctx,
    po, ps, pr, s2, r2, s3, r3, mine, s4, r4,
    in_sem, a1s, a1r, a2s, a2r, a3s, a3r, a4s, a4r,
    bs, br, cs, cr, e1s, e1r, e2s, e2r, e3s, e3r, e4s, e4r,
):
    p = lax.axis_index("pipe")
    y = lax.axis_index("dp")
    t = lax.axis_index("tensor")
    zh, x = p // 4, p % 4
    zl, core = t // 2, t % 2
    z = zh * 4 + zl

    def at(x_, y_, z_, core_):
        return ((z_ // 4) * 4 + x_, y_, (z_ % 4) * 2 + core_)

    sent = []

    def remote(src, dst, send, recv, dev):
        return pltpu.make_async_remote_copy(
            src_ref=src, dst_ref=dst, send_sem=send, recv_sem=recv,
            device_id=dev, device_id_type=MESH,
        )

    def post(src, dst, send, recv, dev):
        copy = remote(src, dst, send, recv, dev)
        copy.start()
        sent.append(copy)

    def arrived(dst, send, recv):
        remote(dst, dst, send, recv, sibling).wait_recv()

    def part(index, size):
        return pl.ds(pl.multiple_of(index * size, size), size)

    zs = [at(x, y, (z + k) % 8, core) for k in range(8)]
    xs = [at((x + k) % 4, y, z, core) for k in range(4)]
    right, left = at(x, (y + 1) % 4, z, core), at(x, (y + 3) % 4, z, core)
    sibling = at(x, y, z, 1 - core)
    hold_x, hold_z = (2 * (p // 2 % 2) + 1 - p % 2 + 2 * (zl % 2)) % 4, 2 * y + zl // 2
    holder = at(hold_x, p // 2, hold_z, core)
    turn = (x + 4 - 2 * (y % 2)) % 4
    owner = (2 * y + 1 - turn % 2, z // 2, (z % 2 * 2 + turn // 2) * 2 + core)

    load_w = pltpu.make_async_copy(w_hbm, wv, in_sem.at[0])
    load_q = pltpu.make_async_copy(q_hbm, q, in_sem.at[1])
    load_g = pltpu.make_async_copy(g_hbm, g, in_sem.at[2])
    for load in (load_w, load_q, load_g):
        load.start()

    barrier = pltpu.get_barrier_semaphore()
    partners = zs[1:] + xs[1:] + [right, left, sibling, holder, owner]
    for dev in partners:
        pl.semaphore_signal(barrier, inc=1, device_id=dev, device_id_type=MESH)

    load_w.wait()

    def lay(i, _):
        block, sub = i // 4, i % 4
        col = (2 * (y % 2) + 1 - block // 8 + 2 * (block // 2 % 2)) % 4
        place = (block % 2) * 8 + col * 2 + block % 8 // 4
        rows = part(place * 4 + sub, 32)
        flat = wv[part(i, 32)].reshape(32, 2 * COLS)
        for n in range(GROUPS):
            w[rows, n * 512:n * 512 + 256] = flat[:, n * 256:(n + 1) * 256]
            w[rows, n * 512 + 256:(n + 1) * 512] = flat[:, COLS + n * 256:COLS + (n + 1) * 256]
        return 0

    lax.fori_loop(0, ROWS // 32, lay, 0)
    pl.semaphore_wait(barrier, len(partners))
    post(
        x_ref, states.at[y, :, part(core * 8 + hold_x * 2 + hold_z % 2, FB)],
        a1s.at[0], a1r.at[0], holder,
    )
    own = states.at[z // 2, :, part(core * 8 + x * 2 + z % 2, FB)]
    arrived(own, a1s.at[0], a1r.at[0])
    for k in (1, 7, 2, 6, 3, 5, 4):
        post(own, own, a2s.at[k - 1], a2r.at[k - 1], zs[k])
    order = (0, 1, 3, 2)
    seqs = [(y + j) % 4 for j in range(4)]
    step_seq = [(z // 2 + n) % 4 for n in range(4)]
    step_j = [(z // 2 + n + 4 - y) % 4 for n in range(4)]
    for n in order:
        for u in range(2):
            other = 2 * step_seq[n] + u if n else z + 1 - 2 * (z % 2)
            if n or u:
                block = states.at[step_seq[n], :, part(core * 8 + x * 2 + other % 2, FB)]
                k = (z + 7 - other) % 8
                arrived(block, a2s.at[k], a2r.at[k])
        pair = states.at[step_seq[n], :, part(core * 4 + x, 2 * FB)]
        for k in (2, 1, 3):
            post(pair, pair, a3s.at[k - 1, n], a3r.at[k - 1, n], xs[k])

    def to_sibling(n):
        for k in (1, 3, 2):
            pair = states.at[step_seq[n], :, part(core * 4 + (x + 4 - k) % 4, 2 * FB)]
            arrived(pair, a3s.at[k - 1, n], a3r.at[k - 1, n])
        half = states.at[step_seq[n], :, part(core, HALF)]
        post(half, half, a4s.at[n], a4r.at[n], sibling)

    def all_here(n):
        arrived(states.at[step_seq[n], :, part(1 - core, HALF)], a4s.at[n], a4r.at[n])

    def project(n, step):
        acc = dot(states[step_seq[step]], w[:, n * 512:(n + 1) * 512], ((1,), (0,)))
        for h in range(2):
            kb[n, step_j[step], h] = acc[:, h * 128:(h + 1) * 128]
            vb[n, step_j[step], h] = acc[:, 256 + h * 128:256 + (h + 1) * 128].astype(BF)

    kinds = ((0, kb, mk, kr), (1, vb, mv, vr))

    def send_far(n):
        for i, buf, mid, _ in kinds:
            post(buf.at[n, 2, 0], mid.at[n, 0], bs.at[n, i], br.at[n, i], right)
            post(buf.at[n, 2, 1], mid.at[n, 1], bs.at[n, 2 + i], br.at[n, 2 + i], left)

    def send_plus(n):
        for i, buf, _, last in kinds:
            post(buf.at[n, 1, 1], last.at[n, 0, 1], bs.at[n, 4 + i], br.at[n, 4 + i], right)

    def send_minus(n):
        for i, buf, _, last in kinds:
            post(buf.at[n, 3, 0], last.at[n, 1, 0], bs.at[n, 6 + i], br.at[n, 6 + i], left)

    def merge(n, h):
        j, dev = ((1, right), (3, left))[h]
        arrived(mk.at[n, h], bs.at[n, 2 * h], br.at[n, 2 * h])
        fk[n, h] = mk[n, h] + kb[n, j, h]
        post(fk.at[n, h], kr.at[n, h, h], bs.at[n, 8 + 2 * h], br.at[n, 8 + 2 * h], dev)
        arrived(mv.at[n, h], bs.at[n, 2 * h + 1], br.at[n, 2 * h + 1])
        fv[n, h] = (mv[n, h].astype(F32) + vb[n, j, h].astype(F32)).astype(BF)
        post(fv.at[n, h], vr.at[n, h, h], bs.at[n, 9 + 2 * h], br.at[n, 9 + 2 * h], dev)

    def once(step, j, act):
        before = len(sent)
        pl.when(step_j[step] == j)(act)
        del sent[before:]

    def merges(step, groups):
        for h, j in enumerate((1, 3)):
            once(step, j, lambda: [merge(n, h) for n in groups].clear())

    factor = 1.0 / math.sqrt(HEAD_DIM)

    def one_head(n, h):
        live = lax.broadcasted_iota(jnp.int32, (TOK, DEC), 0) < len_ref[0]
        cols = slice((2 * n + h) * HEAD_DIM, (2 * n + h + 1) * HEAD_DIM)
        keys = kb[n, 0, h] + kr[n, 0, h] + kr[n, 1, h]
        values = vb[n, 0, h].astype(F32) + vr[n, 0, h].astype(F32) + vr[n, 1, h].astype(F32)
        k1 = keys.astype(BF)
        rest = keys - k1.astype(F32)
        k2 = rest.astype(BF)
        k3 = (rest - k2.astype(F32)).astype(BF)
        v1 = values.astype(BF)
        v2 = (values - v1.astype(F32)).astype(BF)
        qh, gh = q[:, cols], g[:, cols]
        nt, nn, tn = ((1,), (1,)), ((1,), (0,)), ((0,), (0,))
        scores = (dot(k3, qh, nt) + dot(k2, qh, nt) + dot(k1, qh, nt)) * factor
        scores = jnp.where(live, scores, -1e30)
        top = jnp.max(scores, axis=0, keepdims=True)
        expd = jnp.exp(scores - top)
        probs = expd / jnp.sum(expd, axis=0, keepdims=True)
        attn = probs.astype(BF)
        ctx[:, cols] = (dot(attn, v2, tn) + dot(attn, v1, tn)).astype(BF)
        probs_grad = dot(v2, gh, nt) + dot(v1, gh, nt)
        row_dots = jnp.sum(probs * probs_grad, axis=0, keepdims=True)
        score_grad = (probs * (probs_grad - row_dots) * factor).astype(BF)
        lanes = slice(h * HEAD_DIM, (h + 1) * HEAD_DIM)
        kvg[n, 0, 0, :, lanes] = dot(score_grad, qh, nn).astype(BF)
        kvg[n, 0, 1, :, lanes] = dot(attn, gh, nn).astype(BF)

    def attend(n):
        for i, last in enumerate((kr, vr)):
            arrived(last.at[n, 0, 1], bs.at[n, 4 + i], br.at[n, 4 + i])
            arrived(last.at[n, 1, 0], bs.at[n, 6 + i], br.at[n, 6 + i])
            for h in range(2):
                c = 8 + 2 * h + i
                arrived(last.at[n, h, h], bs.at[n, c], br.at[n, c])
        for h in range(2):
            one_head(n, h)
        post(kvg.at[n, 0], kvg.at[n, 3], cs.at[n, 0], cr.at[n, 0], right)
        post(kvg.at[n, 0], kvg.at[n, 1], cs.at[n, 1], cr.at[n, 1], left)

    def pass_on(n):
        arrived(kvg.at[n, 3], cs.at[n, 0], cr.at[n, 0])
        post(kvg.at[n, 3, 0], kvg.at[n, 2, 0], cs.at[n, 2], cr.at[n, 2], right)
        arrived(kvg.at[n, 1], cs.at[n, 1], cr.at[n, 1])
        post(kvg.at[n, 1, 1], kvg.at[n, 2, 1], cs.at[n, 3], cr.at[n, 3], left)

    def far_here(n):
        for h in range(2):
            arrived(kvg.at[n, 2, h], cs.at[n, 2 + h], cr.at[n, 2 + h])

    def early_terms(i, _):
        rows = part(i, 512)
        rhs = jnp.concatenate(
            [kvg[n, :, h].reshape(4 * TOK, 256) for n in range(2) for h in range(2)], axis=1
        )
        acc = dot(w[rows, 0:1024], rhs, ((1,), (1,)))
        for j in range(4):
            po[j, rows, :] = acc[:, j * TOK:(j + 1) * TOK]
        return 0

    def late_terms(half, c, size, js):
        rows = part(half * (HALF // size) + c, size)
        rhs = jnp.concatenate(
            [
                jnp.concatenate([kvg[n, j, h] for j in js], axis=0)
                for n in range(2, GROUPS) for h in range(2)
            ],
            axis=1,
        )
        acc = dot(w[rows, 1024:2048], rhs, ((1,), (1,)))
        return [po[j, rows, :] + acc[:, i * TOK:(i + 1) * TOK] for i, j in enumerate(js)]

    for step in order:
        to_sibling(step)
        all_here(step)
        for n in range(GROUPS):
            project(n, step)
            for j, act in ((2, send_far), (1, send_plus), (3, send_minus)):
                once(step, j, lambda: act(n))
    for step in order[:3]:
        merges(step, range(GROUPS))
    merges(order[3], (0, 1))
    load_q.wait()
    load_g.wait()
    attend(0)
    merges(order[3], (2,))
    attend(1)
    merges(order[3], (3,))
    pass_on(0)
    attend(2)
    pass_on(1)
    attend(3)
    save_ctx = pltpu.make_async_copy(ctx, ctx_hbm, in_sem.at[3])
    save_ctx.start()
    pass_on(2)
    far_here(0)
    far_here(1)
    lax.fori_loop(0, ROWS // 512, early_terms, 0)

    def over_cores(js):
        size = 2 * FB if js == (2,) else HALF
        parts = [(k, (x + k) % 4) for k in (2, 1, 3, 0)] if js == (2,) else [(0, 0)]
        for k, c in parts:
            rows = part(c, size)
            for j, terms in zip(js, late_terms(1 - core, c, size, js)):
                ps[j, rows, :] = terms.astype(BF)
                post(ps.at[j, rows], pr.at[j, rows], e1s.at[j, k], e1r.at[j, k], sibling)
        for _, c in parts:
            for j, terms in zip(js, late_terms(core, c, size, js)):
                po[j, part(core * (HALF // size) + c, size), :] = terms

    def over_x(j):
        if j != 2:
            arrived(pr.at[j], e1s.at[j, 0], e1r.at[j, 0])
        for k in (2, 1, 3, 0):
            c = (x + k) % 4
            rows, own_rows = part(c, 2 * FB), part(core * 4 + c, 2 * FB)
            if j == 2:
                arrived(pr.at[j, rows], e1s.at[j, k], e1r.at[j, k])
            both = po[j, own_rows, :] + pr[j, rows, :].astype(F32)
            if k:
                s2[j, k - 1] = both.astype(BF)
                post(
                    s2.at[j, k - 1], r2.at[k - 1, j], e2s.at[k - 1, j], e2r.at[k - 1, j], xs[k]
                )
            else:
                po[j, own_rows, :] = both

    def to_z(j, u):
        to = 2 * seqs[j] + u
        k = jnp.minimum((z + 7 - to) % 8, 6)
        return to != z, remote(
            s3.at[j, u], r3.at[k], e3s.at[2 * j + u], e3r.at[k], at(x, y, to, core)
        )

    def over_z(j):
        total = po[j, part(core * 4 + x, 2 * FB), :]
        for k in (1, 3, 2):
            arrived(r2.at[k - 1, j], e2s.at[k - 1, j], e2r.at[k - 1, j])
            total += r2[k - 1, j].astype(F32)
        s3[j] = total.reshape(2, FB, TOK).astype(BF)
        for u in range(2):
            away, copy = to_z(j, u)

            @pl.when(away)
            def _():
                copy.start()

            @pl.when(jnp.logical_not(away))
            def _():
                mine[...] = total[u * FB:(u + 1) * FB]

    over_cores((0,))
    pass_on(3)
    over_cores((1, 3))
    over_x(0)
    over_x(1)
    over_x(3)
    far_here(2)
    far_here(3)
    over_cores((2,))
    over_z(0)
    over_z(1)
    over_z(3)
    over_x(2)
    over_z(2)
    total = mine[...]
    for k in (0, 6, 1, 5, 2, 4, 3):
        arrived(r3.at[k], e3s.at[k], e3r.at[k])
        total += r3[k].astype(F32)
    s4[...] = total.T.astype(BF)
    post(s4, r4, e4s.at[0], e4r.at[0], owner)
    arrived(r4, e4s.at[0], e4r.at[0])
    out_ref[...] = r4[...].astype(F32)

    save_ctx.wait()
    for copy in sent:
        copy.wait_send()
    for n in range(GROUPS):
        for i in range(12):
            buf = (kb, vb)[i % 2].at[n, 0, 0]
            remote(buf, buf, bs.at[n, i], br.at[n, i], sibling).wait_send()
    for j in range(4):
        for u in range(2):
            away, copy = to_z(j, u)

            @pl.when(away)
            def _():
                copy.wait_send()


def on_device(enc_states, enc_len, queries, kv_weight, ctx_grad):
    any_spec = pl.BlockSpec(memory_space=pl.ANY)
    vmem = pltpu.VMEM
    dma = lambda *n: pltpu.SemaphoreType.DMA(n)
    context, enc_grad = pl.pallas_call(
        kernel,
        out_shape=(
            jax.ShapeDtypeStruct((DEC, COLS), BF),
            jax.ShapeDtypeStruct((TOK, FB), F32),
        ),
        in_specs=[any_spec, pl.BlockSpec(memory_space=pltpu.SMEM)] + [any_spec] * 3,
        out_specs=(any_spec, pl.BlockSpec(memory_space=pltpu.VMEM)),
        scratch_shapes=[
            vmem((4, TOK, ROWS), BF),
            vmem((ROWS, 2, COLS), BF),
            vmem((ROWS, 2 * COLS), BF),
            vmem((DEC, COLS), BF),
            vmem((DEC, COLS), BF),
            vmem((GROUPS, 4, 2, TOK, HEAD_DIM), F32),
            vmem((GROUPS, 4, 2, TOK, HEAD_DIM), BF),
            vmem((GROUPS, 2, TOK, HEAD_DIM), F32),
            vmem((GROUPS, 2, TOK, HEAD_DIM), BF),
            vmem((GROUPS, 2, TOK, HEAD_DIM), F32),
            vmem((GROUPS, 2, TOK, HEAD_DIM), BF),
            vmem((GROUPS, 2, 2, TOK, HEAD_DIM), F32),
            vmem((GROUPS, 2, 2, TOK, HEAD_DIM), BF),
            vmem((GROUPS, 4, 2, TOK, 2 * HEAD_DIM), BF),
            vmem((DEC, COLS), BF),
            vmem((4, ROWS, TOK), F32),
            vmem((4, HALF, TOK), BF),
            vmem((4, HALF, TOK), BF),
            vmem((4, 3, 2 * FB, TOK), BF),
            vmem((3, 4, 2 * FB, TOK), BF),
            vmem((4, 2, FB, TOK), BF),
            vmem((7, FB, TOK), BF),
            vmem((FB, TOK), F32),
            vmem((TOK, FB), BF),
            vmem((TOK, FB), BF),
            dma(4), dma(1), dma(1), dma(7), dma(7), dma(3, 4), dma(3, 4), dma(4), dma(4),
            dma(GROUPS, 12), dma(GROUPS, 12), dma(GROUPS, 4), dma(GROUPS, 4), dma(4, 4), dma(4, 4),
            dma(3, 4), dma(3, 4), dma(8), dma(7), dma(1), dma(1),
        ],
        compiler_params=pltpu.CompilerParams(
            collective_id=0, has_side_effects=True, vmem_limit_bytes=48 * 2**20
        ),
    )(
        enc_states[0],
        enc_len,
        queries[0, 0],
        kv_weight[0],
        ctx_grad[0, 0],
    )
    return (context[None, None], enc_grad[None])


def solution(mesh):
    return jax.shard_map(
        on_device,
        mesh=mesh,
        in_specs=(
            P("dp", None, ("pipe", "tensor")),
            P("dp"),
            P("pipe", "dp", None, "tensor"),
            P("pipe", "dp", None, "tensor"),
            P("pipe", "dp", None, "tensor"),
        ),
        out_specs=(P("pipe", "dp", None, "tensor"), P("dp", None, ("pipe", "tensor"))),
        check_vma=False,
    )
```

```python
import math

import jax
import jax.numpy as jnp
from jax import lax
from jax.experimental import pallas as pl
from jax.experimental.pallas import tpu as pltpu
from jax.sharding import PartitionSpec as P

HEAD_DIM = 128
TOK = 128
FB = 128
HEADS_HERE = 8
GROUPS = 4
COLS = HEADS_HERE * HEAD_DIM
DEC = 256
ROWS = 2048
HALF = ROWS // 2
BF = jnp.bfloat16
F32 = jnp.float32
MESH = pl.DeviceIdType.MESH


def dot(a, b, dims):
    return lax.dot_general(a, b, (dims, ((), ())), preferred_element_type=F32)


def kernel(
    x_ref, len_ref, q_hbm, w_hbm, g_hbm, ctx_hbm, out_ref,
    states, wv, w, q, g, kb, vb, mk, mv, fk, fv, kr, vr, kvg, ctx,
    po, ps, pr, s2, r2, s3, r3, mine, s4, r4,
    in_sem, a1s, a1r, a2s, a2r, a3s, a3r, a4s, a4r,
    bs, br, cs, cr, e1s, e1r, e2s, e2r, e3s, e3r, e4s, e4r,
):
    p = lax.axis_index("pipe")
    y = lax.axis_index("dp")
    t = lax.axis_index("tensor")
    zh, x = p // 4, p % 4
    zl, core = t // 2, t % 2
    z = zh * 4 + zl

    def at(x_, y_, z_, core_):
        return ((z_ // 4) * 4 + x_, y_, (z_ % 4) * 2 + core_)

    sent = []

    def remote(src, dst, send, recv, dev):
        return pltpu.make_async_remote_copy(
            src_ref=src, dst_ref=dst, send_sem=send, recv_sem=recv,
            device_id=dev, device_id_type=MESH,
        )

    def post(src, dst, send, recv, dev):
        copy = remote(src, dst, send, recv, dev)
        copy.start()
        sent.append(copy)

    def arrived(dst, send, recv):
        remote(dst, dst, send, recv, sibling).wait_recv()

    def part(index, size):
        return pl.ds(pl.multiple_of(index * size, size), size)

    zs = [at(x, y, (z + k) % 8, core) for k in range(8)]
    xs = [at((x + k) % 4, y, z, core) for k in range(4)]
    right, left = at(x, (y + 1) % 4, z, core), at(x, (y + 3) % 4, z, core)
    sibling = at(x, y, z, 1 - core)
    hold_x, hold_z = (2 * (p // 2 % 2) + 1 - p % 2 + 2 * (zl % 2)) % 4, 2 * y + zl // 2
    holder = at(hold_x, p // 2, hold_z, core)
    turn = (x + 4 - 2 * (y % 2)) % 4
    owner = (2 * y + 1 - turn % 2, z // 2, (z % 2 * 2 + turn // 2) * 2 + core)

    load_w = pltpu.make_async_copy(w_hbm, wv, in_sem.at[0])
    load_q = pltpu.make_async_copy(q_hbm, q, in_sem.at[1])
    load_g = pltpu.make_async_copy(g_hbm, g, in_sem.at[2])
    for load in (load_w, load_q, load_g):
        load.start()

    barrier = pltpu.get_barrier_semaphore()
    partners = zs[1:] + xs[1:] + [right, left, sibling, holder, owner]
    for dev in partners:
        pl.semaphore_signal(barrier, inc=1, device_id=dev, device_id_type=MESH)

    load_w.wait()

    def lay(i, _):
        block, sub = i // 4, i % 4
        col = (2 * (y % 2) + 1 - block // 8 + 2 * (block // 2 % 2)) % 4
        place = (block % 2) * 8 + col * 2 + block % 8 // 4
        rows = part(place * 4 + sub, 32)
        flat = wv[part(i, 32)].reshape(32, 2 * COLS)
        for n in range(GROUPS):
            w[rows, n * 512:n * 512 + 256] = flat[:, n * 256:(n + 1) * 256]
            w[rows, n * 512 + 256:(n + 1) * 512] = flat[:, COLS + n * 256:COLS + (n + 1) * 256]
        return 0

    lax.fori_loop(0, ROWS // 32, lay, 0)
    pl.semaphore_wait(barrier, len(partners))
    post(
        x_ref, states.at[y, :, part(core * 8 + hold_x * 2 + hold_z % 2, FB)],
        a1s.at[0], a1r.at[0], holder,
    )
    own = states.at[z // 2, :, part(core * 8 + x * 2 + z % 2, FB)]
    arrived(own, a1s.at[0], a1r.at[0])
    for k in (1, 7, 2, 6, 3, 5, 4):
        post(own, own, a2s.at[k - 1], a2r.at[k - 1], zs[k])
    order = (0, 1, 3, 2)
    seqs = [(y + j) % 4 for j in range(4)]
    step_seq = [(z // 2 + n) % 4 for n in range(4)]
    step_j = [(z // 2 + n + 4 - y) % 4 for n in range(4)]
    for n in order:
        for u in range(2):
            other = 2 * step_seq[n] + u if n else z + 1 - 2 * (z % 2)
            if n or u:
                block = states.at[step_seq[n], :, part(core * 8 + x * 2 + other % 2, FB)]
                k = (z + 7 - other) % 8
                arrived(block, a2s.at[k], a2r.at[k])
        pair = states.at[step_seq[n], :, part(core * 4 + x, 2 * FB)]
        for k in (2, 1, 3):
            post(pair, pair, a3s.at[k - 1, n], a3r.at[k - 1, n], xs[k])

    def to_sibling(n):
        for k in (1, 3, 2):
            pair = states.at[step_seq[n], :, part(core * 4 + (x + 4 - k) % 4, 2 * FB)]
            arrived(pair, a3s.at[k - 1, n], a3r.at[k - 1, n])
        half = states.at[step_seq[n], :, part(core, HALF)]
        post(half, half, a4s.at[n], a4r.at[n], sibling)

    def all_here(n):
        arrived(states.at[step_seq[n], :, part(1 - core, HALF)], a4s.at[n], a4r.at[n])

    def project(n, step):
        acc = dot(states[step_seq[step]], w[:, n * 512:(n + 1) * 512], ((1,), (0,)))
        for h in range(2):
            kb[n, step_j[step], h] = acc[:, h * 128:(h + 1) * 128]
            vb[n, step_j[step], h] = acc[:, 256 + h * 128:256 + (h + 1) * 128].astype(BF)

    kinds = ((0, kb, mk, kr), (1, vb, mv, vr))

    def send_far(n):
        for i, buf, mid, _ in kinds:
            post(buf.at[n, 2, 0], mid.at[n, 0], bs.at[n, i], br.at[n, i], right)
            post(buf.at[n, 2, 1], mid.at[n, 1], bs.at[n, 2 + i], br.at[n, 2 + i], left)

    def send_plus(n):
        for i, buf, _, last in kinds:
            post(buf.at[n, 1, 1], last.at[n, 0, 1], bs.at[n, 4 + i], br.at[n, 4 + i], right)

    def send_minus(n):
        for i, buf, _, last in kinds:
            post(buf.at[n, 3, 0], last.at[n, 1, 0], bs.at[n, 6 + i], br.at[n, 6 + i], left)

    def merge(n, h):
        j, dev = ((1, right), (3, left))[h]
        arrived(mk.at[n, h], bs.at[n, 2 * h], br.at[n, 2 * h])
        fk[n, h] = mk[n, h] + kb[n, j, h]
        post(fk.at[n, h], kr.at[n, h, h], bs.at[n, 8 + 2 * h], br.at[n, 8 + 2 * h], dev)
        arrived(mv.at[n, h], bs.at[n, 2 * h + 1], br.at[n, 2 * h + 1])
        fv[n, h] = (mv[n, h].astype(F32) + vb[n, j, h].astype(F32)).astype(BF)
        post(fv.at[n, h], vr.at[n, h, h], bs.at[n, 9 + 2 * h], br.at[n, 9 + 2 * h], dev)

    def once(step, j, act):
        before = len(sent)
        pl.when(step_j[step] == j)(act)
        del sent[before:]

    def merges(step, groups):
        for h, j in enumerate((1, 3)):
            once(step, j, lambda: [merge(n, h) for n in groups].clear())

    factor = 1.0 / math.sqrt(HEAD_DIM)

    def one_head(n, h):
        live = lax.broadcasted_iota(jnp.int32, (TOK, DEC), 0) < len_ref[0]
        cols = slice((2 * n + h) * HEAD_DIM, (2 * n + h + 1) * HEAD_DIM)
        keys = kb[n, 0, h] + kr[n, 0, h] + kr[n, 1, h]
        values = vb[n, 0, h].astype(F32) + vr[n, 0, h].astype(F32) + vr[n, 1, h].astype(F32)
        k1 = keys.astype(BF)
        rest = keys - k1.astype(F32)
        k2 = rest.astype(BF)
        k3 = (rest - k2.astype(F32)).astype(BF)
        v1 = values.astype(BF)
        v2 = (values - v1.astype(F32)).astype(BF)
        qh, gh = q[:, cols], g[:, cols]
        nt, nn, tn = ((1,), (1,)), ((1,), (0,)), ((0,), (0,))
        scores = (dot(k3, qh, nt) + dot(k2, qh, nt) + dot(k1, qh, nt)) * factor
        scores = jnp.where(live, scores, -1e30)
        top = jnp.max(scores, axis=0, keepdims=True)
        expd = jnp.exp(scores - top)
        probs = expd / jnp.sum(expd, axis=0, keepdims=True)
        attn = probs.astype(BF)
        ctx[:, cols] = (dot(attn, v2, tn) + dot(attn, v1, tn)).astype(BF)
        probs_grad = dot(v2, gh, nt) + dot(v1, gh, nt)
        row_dots = jnp.sum(probs * probs_grad, axis=0, keepdims=True)
        score_grad = (probs * (probs_grad - row_dots) * factor).astype(BF)
        lanes = slice(h * HEAD_DIM, (h + 1) * HEAD_DIM)
        kvg[n, 0, 0, :, lanes] = dot(score_grad, qh, nn).astype(BF)
        kvg[n, 0, 1, :, lanes] = dot(attn, gh, nn).astype(BF)

    def attend(n):
        for i, last in enumerate((kr, vr)):
            arrived(last.at[n, 0, 1], bs.at[n, 4 + i], br.at[n, 4 + i])
            arrived(last.at[n, 1, 0], bs.at[n, 6 + i], br.at[n, 6 + i])
            for h in range(2):
                c = 8 + 2 * h + i
                arrived(last.at[n, h, h], bs.at[n, c], br.at[n, c])
        for h in range(2):
            one_head(n, h)
        post(kvg.at[n, 0], kvg.at[n, 3], cs.at[n, 0], cr.at[n, 0], right)
        post(kvg.at[n, 0], kvg.at[n, 1], cs.at[n, 1], cr.at[n, 1], left)

    def pass_on(n):
        arrived(kvg.at[n, 3], cs.at[n, 0], cr.at[n, 0])
        post(kvg.at[n, 3, 0], kvg.at[n, 2, 0], cs.at[n, 2], cr.at[n, 2], right)
        arrived(kvg.at[n, 1], cs.at[n, 1], cr.at[n, 1])
        post(kvg.at[n, 1, 1], kvg.at[n, 2, 1], cs.at[n, 3], cr.at[n, 3], left)

    def far_here(n):
        for h in range(2):
            arrived(kvg.at[n, 2, h], cs.at[n, 2 + h], cr.at[n, 2 + h])

    def early_terms(i, _):
        rows = part(i, 512)
        rhs = jnp.concatenate(
            [kvg[n, :, h].reshape(4 * TOK, 256) for n in range(2) for h in range(2)], axis=1
        )
        acc = dot(w[rows, 0:1024], rhs, ((1,), (1,)))
        for j in range(4):
            po[j, rows, :] = acc[:, j * TOK:(j + 1) * TOK]
        return 0

    def late_terms(half, c, size, js):
        rows = part(half * (HALF // size) + c, size)
        rhs = jnp.concatenate(
            [
                jnp.concatenate([kvg[n, j, h] for j in js], axis=0)
                for n in range(2, GROUPS) for h in range(2)
            ],
            axis=1,
        )
        acc = dot(w[rows, 1024:2048], rhs, ((1,), (1,)))
        return [po[j, rows, :] + acc[:, i * TOK:(i + 1) * TOK] for i, j in enumerate(js)]

    for step in order:
        to_sibling(step)
        all_here(step)
        for n in range(GROUPS):
            project(n, step)
            for j, act in ((2, send_far), (1, send_plus), (3, send_minus)):
                once(step, j, lambda: act(n))
    for step in order[:3]:
        merges(step, range(GROUPS))
    merges(order[3], (0, 1))
    load_q.wait()
    load_g.wait()
    attend(0)
    merges(order[3], (2,))
    attend(1)
    merges(order[3], (3,))
    pass_on(0)
    attend(2)
    pass_on(1)
    attend(3)
    save_ctx = pltpu.make_async_copy(ctx, ctx_hbm, in_sem.at[3])
    save_ctx.start()
    pass_on(2)
    far_here(0)
    far_here(1)
    lax.fori_loop(0, ROWS // 512, early_terms, 0)

    def over_cores(js):
        size = 2 * FB if js == (2,) else HALF
        parts = [(k, (x + k) % 4) for k in (2, 1, 3, 0)] if js == (2,) else [(0, 0)]
        for k, c in parts:
            rows = part(c, size)
            for j, terms in zip(js, late_terms(1 - core, c, size, js)):
                ps[j, rows, :] = terms.astype(BF)
                post(ps.at[j, rows], pr.at[j, rows], e1s.at[j, k], e1r.at[j, k], sibling)
        for _, c in parts:
            for j, terms in zip(js, late_terms(core, c, size, js)):
                po[j, part(core * (HALF // size) + c, size), :] = terms

    def over_x(j):
        if j != 2:
            arrived(pr.at[j], e1s.at[j, 0], e1r.at[j, 0])
        for k in (2, 1, 3, 0):
            c = (x + k) % 4
            rows, own_rows = part(c, 2 * FB), part(core * 4 + c, 2 * FB)
            if j == 2:
                arrived(pr.at[j, rows], e1s.at[j, k], e1r.at[j, k])
            both = po[j, own_rows, :] + pr[j, rows, :].astype(F32)
            if k:
                s2[j, k - 1] = both.astype(BF)
                post(
                    s2.at[j, k - 1], r2.at[k - 1, j], e2s.at[k - 1, j], e2r.at[k - 1, j], xs[k]
                )
            else:
                po[j, own_rows, :] = both

    def to_z(j, u):
        to = 2 * seqs[j] + u
        k = jnp.minimum((z + 7 - to) % 8, 6)
        return to != z, remote(
            s3.at[j, u], r3.at[k], e3s.at[2 * j + u], e3r.at[k], at(x, y, to, core)
        )

    def over_z(j):
        total = po[j, part(core * 4 + x, 2 * FB), :]
        for k in (1, 3, 2):
            arrived(r2.at[k - 1, j], e2s.at[k - 1, j], e2r.at[k - 1, j])
            total += r2[k - 1, j].astype(F32)
        s3[j] = total.reshape(2, FB, TOK).astype(BF)
        for u in range(2):
            away, copy = to_z(j, u)

            @pl.when(away)
            def _():
                copy.start()

            @pl.when(jnp.logical_not(away))
            def _():
                mine[...] = total[u * FB:(u + 1) * FB]

    pass_on(3)
    over_cores((1, 3))
    over_cores((0,))
    over_x(1)
    over_x(3)
    over_x(0)
    far_here(2)
    far_here(3)
    over_cores((2,))
    over_x(2)
    over_z(1)
    over_z(3)
    over_z(0)
    over_z(2)
    total = mine[...]
    for k in (0, 6, 1, 5, 2, 4, 3):
        arrived(r3.at[k], e3s.at[k], e3r.at[k])
        total += r3[k].astype(F32)
    s4[...] = total.T.astype(BF)
    post(s4, r4, e4s.at[0], e4r.at[0], owner)
    arrived(r4, e4s.at[0], e4r.at[0])
    out_ref[...] = r4[...].astype(F32)

    save_ctx.wait()
    for copy in sent:
        copy.wait_send()
    for n in range(GROUPS):
        for i in range(12):
            buf = (kb, vb)[i % 2].at[n, 0, 0]
            remote(buf, buf, bs.at[n, i], br.at[n, i], sibling).wait_send()
    for j in range(4):
        for u in range(2):
            away, copy = to_z(j, u)

            @pl.when(away)
            def _():
                copy.wait_send()


def on_device(enc_states, enc_len, queries, kv_weight, ctx_grad):
    any_spec = pl.BlockSpec(memory_space=pl.ANY)
    vmem = pltpu.VMEM
    dma = lambda *n: pltpu.SemaphoreType.DMA(n)
    context, enc_grad = pl.pallas_call(
        kernel,
        out_shape=(
            jax.ShapeDtypeStruct((DEC, COLS), BF),
            jax.ShapeDtypeStruct((TOK, FB), F32),
        ),
        in_specs=[any_spec, pl.BlockSpec(memory_space=pltpu.SMEM)] + [any_spec] * 3,
        out_specs=(any_spec, pl.BlockSpec(memory_space=pltpu.VMEM)),
        scratch_shapes=[
            vmem((4, TOK, ROWS), BF),
            vmem((ROWS, 2, COLS), BF),
            vmem((ROWS, 2 * COLS), BF),
            vmem((DEC, COLS), BF),
            vmem((DEC, COLS), BF),
            vmem((GROUPS, 4, 2, TOK, HEAD_DIM), F32),
            vmem((GROUPS, 4, 2, TOK, HEAD_DIM), BF),
            vmem((GROUPS, 2, TOK, HEAD_DIM), F32),
            vmem((GROUPS, 2, TOK, HEAD_DIM), BF),
            vmem((GROUPS, 2, TOK, HEAD_DIM), F32),
            vmem((GROUPS, 2, TOK, HEAD_DIM), BF),
            vmem((GROUPS, 2, 2, TOK, HEAD_DIM), F32),
            vmem((GROUPS, 2, 2, TOK, HEAD_DIM), BF),
            vmem((GROUPS, 4, 2, TOK, 2 * HEAD_DIM), BF),
            vmem((DEC, COLS), BF),
            vmem((4, ROWS, TOK), F32),
            vmem((4, HALF, TOK), BF),
            vmem((4, HALF, TOK), BF),
            vmem((4, 3, 2 * FB, TOK), BF),
            vmem((3, 4, 2 * FB, TOK), BF),
            vmem((4, 2, FB, TOK), BF),
            vmem((7, FB, TOK), BF),
            vmem((FB, TOK), F32),
            vmem((TOK, FB), BF),
            vmem((TOK, FB), BF),
            dma(4), dma(1), dma(1), dma(7), dma(7), dma(3, 4), dma(3, 4), dma(4), dma(4),
            dma(GROUPS, 12), dma(GROUPS, 12), dma(GROUPS, 4), dma(GROUPS, 4), dma(4, 4), dma(4, 4),
            dma(3, 4), dma(3, 4), dma(8), dma(7), dma(1), dma(1),
        ],
        compiler_params=pltpu.CompilerParams(
            collective_id=0, has_side_effects=True, vmem_limit_bytes=48 * 2**20
        ),
    )(
        enc_states[0],
        enc_len,
        queries[0, 0],
        kv_weight[0],
        ctx_grad[0, 0],
    )
    return (context[None, None], enc_grad[None])


def solution(mesh):
    return jax.shard_map(
        on_device,
        mesh=mesh,
        in_specs=(
            P("dp", None, ("pipe", "tensor")),
            P("dp"),
            P("pipe", "dp", None, "tensor"),
            P("pipe", "dp", None, "tensor"),
            P("pipe", "dp", None, "tensor"),
        ),
        out_specs=(P("pipe", "dp", None, "tensor"), P("dp", None, ("pipe", "tensor"))),
        check_vma=False,
    )
```

```python
import math

import jax
import jax.numpy as jnp
from jax import lax
from jax.experimental import pallas as pl
from jax.experimental.pallas import tpu as pltpu
from jax.sharding import PartitionSpec as P

HEAD_DIM = 128
TOK = 128
FB = 128
HEADS_HERE = 8
GROUPS = 4
COLS = HEADS_HERE * HEAD_DIM
DEC = 256
ROWS = 2048
HALF = ROWS // 2
BF = jnp.bfloat16
F32 = jnp.float32
MESH = pl.DeviceIdType.MESH


def dot(a, b, dims):
    return lax.dot_general(a, b, (dims, ((), ())), preferred_element_type=F32)


def kernel(
    x_ref, len_ref, q_hbm, w_hbm, g_hbm, ctx_hbm, out_ref,
    states, wv, w, q, g, kb, vb, mk, mv, fk, fv, kr, vr, kvg, ctx,
    po, ps, pr, s2, r2, s3, r3, mine, s4, r4,
    in_sem, a1s, a1r, a2s, a2r, a3s, a3r, a4s, a4r,
    bs, br, cs, cr, e1s, e1r, e2s, e2r, e3s, e3r, e4s, e4r,
):
    p = lax.axis_index("pipe")
    y = lax.axis_index("dp")
    t = lax.axis_index("tensor")
    zh, x = p // 4, p % 4
    zl, core = t // 2, t % 2
    z = zh * 4 + zl

    def at(x_, y_, z_, core_):
        return ((z_ // 4) * 4 + x_, y_, (z_ % 4) * 2 + core_)

    sent = []

    def remote(src, dst, send, recv, dev):
        return pltpu.make_async_remote_copy(
            src_ref=src, dst_ref=dst, send_sem=send, recv_sem=recv,
            device_id=dev, device_id_type=MESH,
        )

    def post(src, dst, send, recv, dev):
        copy = remote(src, dst, send, recv, dev)
        copy.start()
        sent.append(copy)

    def arrived(dst, send, recv):
        remote(dst, dst, send, recv, sibling).wait_recv()

    def part(index, size):
        return pl.ds(pl.multiple_of(index * size, size), size)

    zs = [at(x, y, (z + k) % 8, core) for k in range(8)]
    xs = [at((x + k) % 4, y, z, core) for k in range(4)]
    right, left = at(x, (y + 1) % 4, z, core), at(x, (y + 3) % 4, z, core)
    sibling = at(x, y, z, 1 - core)
    hold_x, hold_z = (2 * (p // 2 % 2) + 1 - p % 2 + 2 * (zl % 2)) % 4, 2 * y + zl // 2
    holder = at(hold_x, p // 2, hold_z, core)
    turn = (x + 4 - 2 * (y % 2)) % 4
    owner = (2 * y + 1 - turn % 2, z // 2, (z % 2 * 2 + turn // 2) * 2 + core)

    load_w = pltpu.make_async_copy(w_hbm, wv, in_sem.at[0])
    load_q = pltpu.make_async_copy(q_hbm, q, in_sem.at[1])
    load_g = pltpu.make_async_copy(g_hbm, g, in_sem.at[2])
    for load in (load_w, load_q, load_g):
        load.start()

    barrier = pltpu.get_barrier_semaphore()
    partners = zs[1:] + xs[1:] + [right, left, sibling, holder, owner]
    for dev in partners:
        pl.semaphore_signal(barrier, inc=1, device_id=dev, device_id_type=MESH)

    load_w.wait()

    def lay(i, _):
        block, sub = i // 4, i % 4
        col = (2 * (y % 2) + 1 - block // 8 + 2 * (block // 2 % 2)) % 4
        place = (block % 2) * 8 + col * 2 + block % 8 // 4
        rows = part(place * 4 + sub, 32)
        flat = wv[part(i, 32)].reshape(32, 2 * COLS)
        for n in range(GROUPS):
            w[rows, n * 512:n * 512 + 256] = flat[:, n * 256:(n + 1) * 256]
            w[rows, n * 512 + 256:(n + 1) * 512] = flat[:, COLS + n * 256:COLS + (n + 1) * 256]
        return 0

    lax.fori_loop(0, ROWS // 32, lay, 0)
    pl.semaphore_wait(barrier, len(partners))
    post(
        x_ref, states.at[y, :, part(core * 8 + hold_x * 2 + hold_z % 2, FB)],
        a1s.at[0], a1r.at[0], holder,
    )
    own = states.at[z // 2, :, part(core * 8 + x * 2 + z % 2, FB)]
    arrived(own, a1s.at[0], a1r.at[0])
    for k in (1, 7, 2, 6, 3, 5, 4):
        post(own, own, a2s.at[k - 1], a2r.at[k - 1], zs[k])
    order = (0, 1, 3, 2)
    seqs = [(y + j) % 4 for j in range(4)]
    step_seq = [(z // 2 + n) % 4 for n in range(4)]
    step_j = [(z // 2 + n + 4 - y) % 4 for n in range(4)]
    for n in order:
        for u in range(2):
            other = 2 * step_seq[n] + u if n else z + 1 - 2 * (z % 2)
            if n or u:
                block = states.at[step_seq[n], :, part(core * 8 + x * 2 + other % 2, FB)]
                k = (z + 7 - other) % 8
                arrived(block, a2s.at[k], a2r.at[k])
        pair = states.at[step_seq[n], :, part(core * 4 + x, 2 * FB)]
        for k in (2, 1, 3):
            post(pair, pair, a3s.at[k - 1, n], a3r.at[k - 1, n], xs[k])

    def to_sibling(n):
        for k in (1, 3, 2):
            pair = states.at[step_seq[n], :, part(core * 4 + (x + 4 - k) % 4, 2 * FB)]
            arrived(pair, a3s.at[k - 1, n], a3r.at[k - 1, n])
        half = states.at[step_seq[n], :, part(core, HALF)]
        post(half, half, a4s.at[n], a4r.at[n], sibling)

    def all_here(n):
        arrived(states.at[step_seq[n], :, part(1 - core, HALF)], a4s.at[n], a4r.at[n])

    def project(n, step):
        acc = dot(states[step_seq[step]], w[:, n * 512:(n + 1) * 512], ((1,), (0,)))
        for h in range(2):
            kb[n, step_j[step], h] = acc[:, h * 128:(h + 1) * 128]
            vb[n, step_j[step], h] = acc[:, 256 + h * 128:256 + (h + 1) * 128].astype(BF)

    kinds = ((0, kb, mk, kr), (1, vb, mv, vr))

    def send_far(n):
        for i, buf, mid, _ in kinds:
            post(buf.at[n, 2, 0], mid.at[n, 0], bs.at[n, i], br.at[n, i], right)
            post(buf.at[n, 2, 1], mid.at[n, 1], bs.at[n, 2 + i], br.at[n, 2 + i], left)

    def send_plus(n):
        for i, buf, _, last in kinds:
            post(buf.at[n, 1, 1], last.at[n, 0, 1], bs.at[n, 4 + i], br.at[n, 4 + i], right)

    def send_minus(n):
        for i, buf, _, last in kinds:
            post(buf.at[n, 3, 0], last.at[n, 1, 0], bs.at[n, 6 + i], br.at[n, 6 + i], left)

    def merge(n, h):
        j, dev = ((1, right), (3, left))[h]
        arrived(mk.at[n, h], bs.at[n, 2 * h], br.at[n, 2 * h])
        fk[n, h] = mk[n, h] + kb[n, j, h]
        post(fk.at[n, h], kr.at[n, h, h], bs.at[n, 8 + 2 * h], br.at[n, 8 + 2 * h], dev)
        arrived(mv.at[n, h], bs.at[n, 2 * h + 1], br.at[n, 2 * h + 1])
        fv[n, h] = (mv[n, h].astype(F32) + vb[n, j, h].astype(F32)).astype(BF)
        post(fv.at[n, h], vr.at[n, h, h], bs.at[n, 9 + 2 * h], br.at[n, 9 + 2 * h], dev)

    def once(step, j, act):
        before = len(sent)
        pl.when(step_j[step] == j)(act)
        del sent[before:]

    def merges(step, groups):
        for h, j in enumerate((1, 3)):
            once(step, j, lambda: [merge(n, h) for n in groups].clear())

    factor = 1.0 / math.sqrt(HEAD_DIM)

    def one_head(n, h):
        live = lax.broadcasted_iota(jnp.int32, (TOK, DEC), 0) < len_ref[0]
        cols = slice((2 * n + h) * HEAD_DIM, (2 * n + h + 1) * HEAD_DIM)
        keys = kb[n, 0, h] + kr[n, 0, h] + kr[n, 1, h]
        values = vb[n, 0, h].astype(F32) + vr[n, 0, h].astype(F32) + vr[n, 1, h].astype(F32)
        k1 = keys.astype(BF)
        rest = keys - k1.astype(F32)
        k2 = rest.astype(BF)
        k3 = (rest - k2.astype(F32)).astype(BF)
        v1 = values.astype(BF)
        v2 = (values - v1.astype(F32)).astype(BF)
        qh, gh = q[:, cols], g[:, cols]
        nt, nn, tn = ((1,), (1,)), ((1,), (0,)), ((0,), (0,))
        scores = (dot(k3, qh, nt) + dot(k2, qh, nt) + dot(k1, qh, nt)) * factor
        scores = jnp.where(live, scores, -1e30)
        top = jnp.max(scores, axis=0, keepdims=True)
        expd = jnp.exp(scores - top)
        probs = expd / jnp.sum(expd, axis=0, keepdims=True)
        attn = probs.astype(BF)
        ctx[:, cols] = (dot(attn, v2, tn) + dot(attn, v1, tn)).astype(BF)
        probs_grad = dot(v2, gh, nt) + dot(v1, gh, nt)
        row_dots = jnp.sum(probs * probs_grad, axis=0, keepdims=True)
        score_grad = (probs * (probs_grad - row_dots) * factor).astype(BF)
        lanes = slice(h * HEAD_DIM, (h + 1) * HEAD_DIM)
        kvg[n, 0, 0, :, lanes] = dot(score_grad, qh, nn).astype(BF)
        kvg[n, 0, 1, :, lanes] = dot(attn, gh, nn).astype(BF)

    def attend(n):
        for i, last in enumerate((kr, vr)):
            arrived(last.at[n, 0, 1], bs.at[n, 4 + i], br.at[n, 4 + i])
            arrived(last.at[n, 1, 0], bs.at[n, 6 + i], br.at[n, 6 + i])
            for h in range(2):
                c = 8 + 2 * h + i
                arrived(last.at[n, h, h], bs.at[n, c], br.at[n, c])
        for h in range(2):
            one_head(n, h)
        post(kvg.at[n, 0], kvg.at[n, 3], cs.at[n, 0], cr.at[n, 0], right)
        post(kvg.at[n, 0], kvg.at[n, 1], cs.at[n, 1], cr.at[n, 1], left)

    def pass_on(n):
        arrived(kvg.at[n, 3], cs.at[n, 0], cr.at[n, 0])
        post(kvg.at[n, 3, 0], kvg.at[n, 2, 0], cs.at[n, 2], cr.at[n, 2], right)
        arrived(kvg.at[n, 1], cs.at[n, 1], cr.at[n, 1])
        post(kvg.at[n, 1, 1], kvg.at[n, 2, 1], cs.at[n, 3], cr.at[n, 3], left)

    def far_here(n):
        for h in range(2):
            arrived(kvg.at[n, 2, h], cs.at[n, 2 + h], cr.at[n, 2 + h])

    def early_terms(i, _):
        rows = part(i, 512)
        rhs = jnp.concatenate(
            [kvg[n, :, h].reshape(4 * TOK, 256) for n in range(2) for h in range(2)], axis=1
        )
        acc = dot(w[rows, 0:1024], rhs, ((1,), (1,)))
        for j in range(4):
            po[j, rows, :] = acc[:, j * TOK:(j + 1) * TOK]
        return 0

    def late_terms(half, c, size, js):
        rows = part(half * (HALF // size) + c, size)
        rhs = jnp.concatenate(
            [
                jnp.concatenate([kvg[n, j, h] for j in js], axis=0)
                for n in range(2, GROUPS) for h in range(2)
            ],
            axis=1,
        )
        acc = dot(w[rows, 1024:2048], rhs, ((1,), (1,)))
        return [po[j, rows, :] + acc[:, i * TOK:(i + 1) * TOK] for i, j in enumerate(js)]

    to_sibling(order[0])
    all_here(order[0])
    for i, step in enumerate(order):
        for n in range(GROUPS):
            project(n, step)
            for j, act in ((2, send_far), (1, send_plus), (3, send_minus)):
                once(step, j, lambda: act(n))
            if n == 1 and i < 3:
                to_sibling(order[i + 1])
        if i == 2:
            merges(order[0], (0, 1))
        if i < 3:
            all_here(order[i + 1])
    merges(order[0], (2, 3))
    for step in order[1:3]:
        merges(step, range(GROUPS))
    merges(order[3], (0, 1))
    load_q.wait()
    load_g.wait()
    attend(0)
    merges(order[3], (2,))
    attend(1)
    merges(order[3], (3,))
    pass_on(0)
    attend(2)
    pass_on(1)
    attend(3)
    save_ctx = pltpu.make_async_copy(ctx, ctx_hbm, in_sem.at[3])
    save_ctx.start()
    pass_on(2)
    far_here(0)
    far_here(1)
    lax.fori_loop(0, ROWS // 512, early_terms, 0)

    def over_cores(js):
        size = 2 * FB if js == (2,) else HALF
        parts = [(k, (x + k) % 4) for k in (2, 1, 3, 0)] if js == (2,) else [(0, 0)]
        for k, c in parts:
            rows = part(c, size)
            for j, terms in zip(js, late_terms(1 - core, c, size, js)):
                ps[j, rows, :] = terms.astype(BF)
                post(ps.at[j, rows], pr.at[j, rows], e1s.at[j, k], e1r.at[j, k], sibling)
        for k, c in parts:
            for j, terms in zip(js, late_terms(core, c, size, js)):
                po[j, part(core * (HALF // size) + c, size), :] = terms
            if js == (2,):
                over_x(2, (k,))

    def over_x(j, places=(2, 1, 3, 0)):
        if j != 2:
            arrived(pr.at[j], e1s.at[j, 0], e1r.at[j, 0])
        for k in places:
            c = (x + k) % 4
            rows, own_rows = part(c, 2 * FB), part(core * 4 + c, 2 * FB)
            if j == 2:
                arrived(pr.at[j, rows], e1s.at[j, k], e1r.at[j, k])
            both = po[j, own_rows, :] + pr[j, rows, :].astype(F32)
            if k:
                s2[j, k - 1] = both.astype(BF)
                post(
                    s2.at[j, k - 1], r2.at[k - 1, j], e2s.at[k - 1, j], e2r.at[k - 1, j], xs[k]
                )
            else:
                po[j, own_rows, :] = both

    def to_z(j, u):
        to = 2 * seqs[j] + u
        k = jnp.minimum((z + 7 - to) % 8, 6)
        return to != z, remote(
            s3.at[j, u], r3.at[k], e3s.at[2 * j + u], e3r.at[k], at(x, y, to, core)
        )

    def over_z(j):
        total = po[j, part(core * 4 + x, 2 * FB), :]
        for k in (1, 3, 2):
            arrived(r2.at[k - 1, j], e2s.at[k - 1, j], e2r.at[k - 1, j])
            total += r2[k - 1, j].astype(F32)
        s3[j] = total.reshape(2, FB, TOK).astype(BF)
        for u in range(2):
            away, copy = to_z(j, u)

            @pl.when(away)
            def _():
                copy.start()

            @pl.when(jnp.logical_not(away))
            def _():
                mine[...] = total[u * FB:(u + 1) * FB]

    pass_on(3)
    over_cores((1, 3))
    over_cores((0,))
    over_x(1)
    over_x(3)
    over_x(0)
    far_here(2)
    far_here(3)
    over_cores((2,))
    over_z(1)
    over_z(3)
    over_z(0)
    over_z(2)
    total = mine[...]
    for k in (0, 6, 1, 5, 2, 4, 3):
        arrived(r3.at[k], e3s.at[k], e3r.at[k])
        total += r3[k].astype(F32)
    s4[...] = total.T.astype(BF)
    post(s4, r4, e4s.at[0], e4r.at[0], owner)
    arrived(r4, e4s.at[0], e4r.at[0])
    out_ref[...] = r4[...].astype(F32)

    save_ctx.wait()
    for copy in sent:
        copy.wait_send()
    for n in range(GROUPS):
        for i in range(12):
            buf = (kb, vb)[i % 2].at[n, 0, 0]
            remote(buf, buf, bs.at[n, i], br.at[n, i], sibling).wait_send()
    for j in range(4):
        for u in range(2):
            away, copy = to_z(j, u)

            @pl.when(away)
            def _():
                copy.wait_send()


def on_device(enc_states, enc_len, queries, kv_weight, ctx_grad):
    any_spec = pl.BlockSpec(memory_space=pl.ANY)
    vmem = pltpu.VMEM
    dma = lambda *n: pltpu.SemaphoreType.DMA(n)
    context, enc_grad = pl.pallas_call(
        kernel,
        out_shape=(
            jax.ShapeDtypeStruct((DEC, COLS), BF),
            jax.ShapeDtypeStruct((TOK, FB), F32),
        ),
        in_specs=[any_spec, pl.BlockSpec(memory_space=pltpu.SMEM)] + [any_spec] * 3,
        out_specs=(any_spec, pl.BlockSpec(memory_space=pltpu.VMEM)),
        scratch_shapes=[
            vmem((4, TOK, ROWS), BF),
            vmem((ROWS, 2, COLS), BF),
            vmem((ROWS, 2 * COLS), BF),
            vmem((DEC, COLS), BF),
            vmem((DEC, COLS), BF),
            vmem((GROUPS, 4, 2, TOK, HEAD_DIM), F32),
            vmem((GROUPS, 4, 2, TOK, HEAD_DIM), BF),
            vmem((GROUPS, 2, TOK, HEAD_DIM), F32),
            vmem((GROUPS, 2, TOK, HEAD_DIM), BF),
            vmem((GROUPS, 2, TOK, HEAD_DIM), F32),
            vmem((GROUPS, 2, TOK, HEAD_DIM), BF),
            vmem((GROUPS, 2, 2, TOK, HEAD_DIM), F32),
            vmem((GROUPS, 2, 2, TOK, HEAD_DIM), BF),
            vmem((GROUPS, 4, 2, TOK, 2 * HEAD_DIM), BF),
            vmem((DEC, COLS), BF),
            vmem((4, ROWS, TOK), F32),
            vmem((4, HALF, TOK), BF),
            vmem((4, HALF, TOK), BF),
            vmem((4, 3, 2 * FB, TOK), BF),
            vmem((3, 4, 2 * FB, TOK), BF),
            vmem((4, 2, FB, TOK), BF),
            vmem((7, FB, TOK), BF),
            vmem((FB, TOK), F32),
            vmem((TOK, FB), BF),
            vmem((TOK, FB), BF),
            dma(4), dma(1), dma(1), dma(7), dma(7), dma(3, 4), dma(3, 4), dma(4), dma(4),
            dma(GROUPS, 12), dma(GROUPS, 12), dma(GROUPS, 4), dma(GROUPS, 4), dma(4, 4), dma(4, 4),
            dma(3, 4), dma(3, 4), dma(8), dma(7), dma(1), dma(1),
        ],
        compiler_params=pltpu.CompilerParams(
            collective_id=0, has_side_effects=True, vmem_limit_bytes=48 * 2**20
        ),
    )(
        enc_states[0],
        enc_len,
        queries[0, 0],
        kv_weight[0],
        ctx_grad[0, 0],
    )
    return (context[None, None], enc_grad[None])


def solution(mesh):
    return jax.shard_map(
        on_device,
        mesh=mesh,
        in_specs=(
            P("dp", None, ("pipe", "tensor")),
            P("dp"),
            P("pipe", "dp", None, "tensor"),
            P("pipe", "dp", None, "tensor"),
            P("pipe", "dp", None, "tensor"),
        ),
        out_specs=(P("pipe", "dp", None, "tensor"), P("dp", None, ("pipe", "tensor"))),
        check_vma=False,
    )
```

```python
import math

import jax
import jax.numpy as jnp
from jax import lax
from jax.experimental import pallas as pl
from jax.experimental.pallas import tpu as pltpu
from jax.sharding import PartitionSpec as P

HEAD_DIM = 128
TOK = 128
FB = 128
HEADS_HERE = 8
GROUPS = 4
COLS = HEADS_HERE * HEAD_DIM
DEC = 256
ROWS = 2048
HALF = ROWS // 2
BF = jnp.bfloat16
F32 = jnp.float32
MESH = pl.DeviceIdType.MESH


def dot(a, b, dims):
    return lax.dot_general(a, b, (dims, ((), ())), preferred_element_type=F32)


def kernel(
    x_ref, len_ref, q_hbm, w_hbm, g_hbm, ctx_hbm, out_ref,
    states, wv, w, q, g, kb, vb, mk, mv, fk, fv, kr, vr, kvg, ctx,
    po, ps, pr, s2, r2, s3, r3, mine, s4, r4,
    in_sem, a1s, a1r, a2s, a2r, a3s, a3r, a4s, a4r,
    bs, br, cs, cr, e1s, e1r, e2s, e2r, e3s, e3r, e4s, e4r,
):
    p = lax.axis_index("pipe")
    y = lax.axis_index("dp")
    t = lax.axis_index("tensor")
    zh, x = p // 4, p % 4
    zl, core = t // 2, t % 2
    z = zh * 4 + zl

    def at(x_, y_, z_, core_):
        return ((z_ // 4) * 4 + x_, y_, (z_ % 4) * 2 + core_)

    sent = []

    def remote(src, dst, send, recv, dev):
        return pltpu.make_async_remote_copy(
            src_ref=src, dst_ref=dst, send_sem=send, recv_sem=recv,
            device_id=dev, device_id_type=MESH,
        )

    def post(src, dst, send, recv, dev):
        copy = remote(src, dst, send, recv, dev)
        copy.start()
        sent.append(copy)

    def arrived(dst, send, recv):
        remote(dst, dst, send, recv, sibling).wait_recv()

    def part(index, size):
        return pl.ds(pl.multiple_of(index * size, size), size)

    zs = [at(x, y, (z + k) % 8, core) for k in range(8)]
    xs = [at((x + k) % 4, y, z, core) for k in range(4)]
    right, left = at(x, (y + 1) % 4, z, core), at(x, (y + 3) % 4, z, core)
    sibling = at(x, y, z, 1 - core)
    hold_x, hold_z = (2 * (p // 2 % 2) + 1 - p % 2 + 2 * (zl % 2)) % 4, 2 * y + zl // 2
    holder = at(hold_x, p // 2, hold_z, core)
    turn = (x + 4 - 2 * (y % 2)) % 4
    owner = (2 * y + 1 - turn % 2, z // 2, (z % 2 * 2 + turn // 2) * 2 + core)

    load_w = pltpu.make_async_copy(w_hbm, wv, in_sem.at[0])
    load_q = pltpu.make_async_copy(q_hbm, q, in_sem.at[1])
    load_g = pltpu.make_async_copy(g_hbm, g, in_sem.at[2])
    for load in (load_w, load_q, load_g):
        load.start()

    barrier = pltpu.get_barrier_semaphore()
    partners = zs[1:] + xs[1:] + [right, left, sibling, holder, owner]
    for dev in partners:
        pl.semaphore_signal(barrier, inc=1, device_id=dev, device_id_type=MESH)

    load_w.wait()

    def lay(i, _):
        block, sub = i // 4, i % 4
        col = (2 * (y % 2) + 1 - block // 8 + 2 * (block // 2 % 2)) % 4
        place = (block % 2) * 8 + col * 2 + block % 8 // 4
        rows = part(place * 4 + sub, 32)
        flat = wv[part(i, 32)].reshape(32, 2 * COLS)
        for n in range(GROUPS):
            w[rows, n * 512:n * 512 + 256] = flat[:, n * 256:(n + 1) * 256]
            w[rows, n * 512 + 256:(n + 1) * 512] = flat[:, COLS + n * 256:COLS + (n + 1) * 256]
        return 0

    lax.fori_loop(0, ROWS // 32, lay, 0)
    pl.semaphore_wait(barrier, len(partners))
    post(
        x_ref, states.at[y, :, part(core * 8 + hold_x * 2 + hold_z % 2, FB)],
        a1s.at[0], a1r.at[0], holder,
    )
    own = states.at[z // 2, :, part(core * 8 + x * 2 + z % 2, FB)]
    arrived(own, a1s.at[0], a1r.at[0])
    for k in (1, 7, 2, 6, 3, 5, 4):
        post(own, own, a2s.at[k - 1], a2r.at[k - 1], zs[k])
    order = (0, 1, 3, 2)
    seqs = [(y + j) % 4 for j in range(4)]
    step_seq = [(z // 2 + n) % 4 for n in range(4)]
    step_j = [(z // 2 + n + 4 - y) % 4 for n in range(4)]
    for n in order:
        for u in range(2):
            other = 2 * step_seq[n] + u if n else z + 1 - 2 * (z % 2)
            if n or u:
                block = states.at[step_seq[n], :, part(core * 8 + x * 2 + other % 2, FB)]
                k = (z + 7 - other) % 8
                arrived(block, a2s.at[k], a2r.at[k])
        pair = states.at[step_seq[n], :, part(core * 4 + x, 2 * FB)]
        for k in (2, 1, 3):
            post(pair, pair, a3s.at[k - 1, n], a3r.at[k - 1, n], xs[k])

    def to_sibling(n):
        for k in (1, 3, 2):
            pair = states.at[step_seq[n], :, part(core * 4 + (x + 4 - k) % 4, 2 * FB)]
            arrived(pair, a3s.at[k - 1, n], a3r.at[k - 1, n])
        half = states.at[step_seq[n], :, part(core, HALF)]
        post(half, half, a4s.at[n], a4r.at[n], sibling)

    def all_here(n):
        arrived(states.at[step_seq[n], :, part(1 - core, HALF)], a4s.at[n], a4r.at[n])

    def project(n, step):
        acc = dot(states[step_seq[step]], w[:, n * 512:(n + 1) * 512], ((1,), (0,)))
        for h in range(2):
            kb[n, step_j[step], h] = acc[:, h * 128:(h + 1) * 128]
            vb[n, step_j[step], h] = acc[:, 256 + h * 128:256 + (h + 1) * 128].astype(BF)

    kinds = ((0, kb, mk, kr), (1, vb, mv, vr))

    def send_far(n):
        for i, buf, mid, _ in kinds:
            post(buf.at[n, 2, 0], mid.at[n, 0], bs.at[n, i], br.at[n, i], right)
            post(buf.at[n, 2, 1], mid.at[n, 1], bs.at[n, 2 + i], br.at[n, 2 + i], left)

    def send_plus(n):
        for i, buf, _, last in kinds:
            post(buf.at[n, 1, 1], last.at[n, 0, 1], bs.at[n, 4 + i], br.at[n, 4 + i], right)

    def send_minus(n):
        for i, buf, _, last in kinds:
            post(buf.at[n, 3, 0], last.at[n, 1, 0], bs.at[n, 6 + i], br.at[n, 6 + i], left)

    def merge(n, h):
        j, dev = ((1, right), (3, left))[h]
        arrived(mk.at[n, h], bs.at[n, 2 * h], br.at[n, 2 * h])
        fk[n, h] = mk[n, h] + kb[n, j, h]
        post(fk.at[n, h], kr.at[n, h, h], bs.at[n, 8 + 2 * h], br.at[n, 8 + 2 * h], dev)
        arrived(mv.at[n, h], bs.at[n, 2 * h + 1], br.at[n, 2 * h + 1])
        fv[n, h] = (mv[n, h].astype(F32) + vb[n, j, h].astype(F32)).astype(BF)
        post(fv.at[n, h], vr.at[n, h, h], bs.at[n, 9 + 2 * h], br.at[n, 9 + 2 * h], dev)

    def once(step, j, act):
        before = len(sent)
        pl.when(step_j[step] == j)(act)
        del sent[before:]

    def merges(step, groups):
        for h, j in enumerate((1, 3)):
            once(step, j, lambda: [merge(n, h) for n in groups].clear())

    factor = 1.0 / math.sqrt(HEAD_DIM)

    def one_head(n, h):
        live = lax.broadcasted_iota(jnp.int32, (TOK, DEC), 0) < len_ref[0]
        cols = slice((2 * n + h) * HEAD_DIM, (2 * n + h + 1) * HEAD_DIM)
        keys = kb[n, 0, h] + kr[n, 0, h] + kr[n, 1, h]
        values = vb[n, 0, h].astype(F32) + vr[n, 0, h].astype(F32) + vr[n, 1, h].astype(F32)
        k1 = keys.astype(BF)
        rest = keys - k1.astype(F32)
        k2 = rest.astype(BF)
        k3 = (rest - k2.astype(F32)).astype(BF)
        v1 = values.astype(BF)
        v2 = (values - v1.astype(F32)).astype(BF)
        qh, gh = q[:, cols], g[:, cols]
        nt, nn, tn = ((1,), (1,)), ((1,), (0,)), ((0,), (0,))
        scores = (dot(k3, qh, nt) + dot(k2, qh, nt) + dot(k1, qh, nt)) * factor
        scores = jnp.where(live, scores, -1e30)
        top = jnp.max(scores, axis=0, keepdims=True)
        expd = jnp.exp(scores - top)
        probs = expd / jnp.sum(expd, axis=0, keepdims=True)
        attn = probs.astype(BF)
        ctx[:, cols] = (dot(attn, v2, tn) + dot(attn, v1, tn)).astype(BF)
        probs_grad = dot(v2, gh, nt) + dot(v1, gh, nt)
        row_dots = jnp.sum(probs * probs_grad, axis=0, keepdims=True)
        score_grad = (probs * (probs_grad - row_dots) * factor).astype(BF)
        lanes = slice(h * HEAD_DIM, (h + 1) * HEAD_DIM)
        kvg[n, 0, 0, :, lanes] = dot(score_grad, qh, nn).astype(BF)
        kvg[n, 0, 1, :, lanes] = dot(attn, gh, nn).astype(BF)

    def attend(n):
        for i, last in enumerate((kr, vr)):
            arrived(last.at[n, 0, 1], bs.at[n, 4 + i], br.at[n, 4 + i])
            arrived(last.at[n, 1, 0], bs.at[n, 6 + i], br.at[n, 6 + i])
            for h in range(2):
                c = 8 + 2 * h + i
                arrived(last.at[n, h, h], bs.at[n, c], br.at[n, c])
        for h in range(2):
            one_head(n, h)
        post(kvg.at[n, 0], kvg.at[n, 3], cs.at[n, 0], cr.at[n, 0], right)
        post(kvg.at[n, 0], kvg.at[n, 1], cs.at[n, 1], cr.at[n, 1], left)

    def pass_on(n):
        arrived(kvg.at[n, 3], cs.at[n, 0], cr.at[n, 0])
        post(kvg.at[n, 3, 0], kvg.at[n, 2, 0], cs.at[n, 2], cr.at[n, 2], right)
        arrived(kvg.at[n, 1], cs.at[n, 1], cr.at[n, 1])
        post(kvg.at[n, 1, 1], kvg.at[n, 2, 1], cs.at[n, 3], cr.at[n, 3], left)

    def far_here(n):
        for h in range(2):
            arrived(kvg.at[n, 2, h], cs.at[n, 2 + h], cr.at[n, 2 + h])

    def early_terms(i, _):
        rows = part(i, 512)
        rhs = jnp.concatenate(
            [kvg[n, :, h].reshape(4 * TOK, 256) for n in range(2) for h in range(2)], axis=1
        )
        acc = dot(w[rows, 0:1024], rhs, ((1,), (1,)))
        for j in range(4):
            po[j, rows, :] = acc[:, j * TOK:(j + 1) * TOK]
        return 0

    def late_terms(half, c, size, js):
        rows = part(half * (HALF // size) + c, size)
        rhs = jnp.concatenate(
            [
                jnp.concatenate([kvg[n, j, h] for j in js], axis=0)
                for n in range(2, GROUPS) for h in range(2)
            ],
            axis=1,
        )
        acc = dot(w[rows, 1024:2048], rhs, ((1,), (1,)))
        return [po[j, rows, :] + acc[:, i * TOK:(i + 1) * TOK] for i, j in enumerate(js)]

    to_sibling(order[0])
    all_here(order[0])
    for i, step in enumerate(order):
        for n in range(GROUPS):
            project(n, step)
            for j, act in ((2, send_far), (1, send_plus), (3, send_minus)):
                once(step, j, lambda: act(n))
            if n == 1 and i < 3:
                to_sibling(order[i + 1])
            if n == 1 and i == 3:
                merges(order[0], (2,))
        if i == 2:
            merges(order[0], (0, 1))
        if i < 3:
            all_here(order[i + 1])
    merges(order[0], (3,))
    for step in order[1:3]:
        merges(step, range(GROUPS))
    merges(order[3], (0, 1))
    load_q.wait()
    load_g.wait()
    attend(0)
    merges(order[3], (2,))
    attend(1)
    merges(order[3], (3,))
    pass_on(0)
    attend(2)
    pass_on(1)
    attend(3)
    save_ctx = pltpu.make_async_copy(ctx, ctx_hbm, in_sem.at[3])
    save_ctx.start()
    pass_on(2)
    far_here(0)
    far_here(1)
    lax.fori_loop(0, ROWS // 512, early_terms, 0)

    def over_cores(js):
        size = 2 * FB if js == (2,) else HALF
        parts = [(k, (x + k) % 4) for k in (2, 1, 3, 0)] if js == (2,) else [(0, 0)]
        for k, c in parts:
            rows = part(c, size)
            for j, terms in zip(js, late_terms(1 - core, c, size, js)):
                ps[j, rows, :] = terms.astype(BF)
                post(ps.at[j, rows], pr.at[j, rows], e1s.at[j, k], e1r.at[j, k], sibling)
        for k, c in parts:
            for j, terms in zip(js, late_terms(core, c, size, js)):
                po[j, part(core * (HALF // size) + c, size), :] = terms
            if js == (2,):
                over_x(2, (k,))

    def over_x(j, places=(2, 1, 3, 0)):
        if j != 2:
            arrived(pr.at[j], e1s.at[j, 0], e1r.at[j, 0])
        for k in places:
            c = (x + k) % 4
            rows, own_rows = part(c, 2 * FB), part(core * 4 + c, 2 * FB)
            if j == 2:
                arrived(pr.at[j, rows], e1s.at[j, k], e1r.at[j, k])
            both = po[j, own_rows, :] + pr[j, rows, :].astype(F32)
            if k:
                s2[j, k - 1] = both.astype(BF)
                post(
                    s2.at[j, k - 1], r2.at[k - 1, j], e2s.at[k - 1, j], e2r.at[k - 1, j], xs[k]
                )
            else:
                po[j, own_rows, :] = both

    def to_z(j, u):
        to = 2 * seqs[j] + u
        k = jnp.minimum((z + 7 - to) % 8, 6)
        return to != z, remote(
            s3.at[j, u], r3.at[k], e3s.at[2 * j + u], e3r.at[k], at(x, y, to, core)
        )

    def over_z(j):
        total = po[j, part(core * 4 + x, 2 * FB), :]
        for k in (1, 3, 2):
            arrived(r2.at[k - 1, j], e2s.at[k - 1, j], e2r.at[k - 1, j])
            total += r2[k - 1, j].astype(F32)
        s3[j] = total.reshape(2, FB, TOK).astype(BF)
        for u in range(2):
            away, copy = to_z(j, u)

            @pl.when(away)
            def _():
                copy.start()

            @pl.when(jnp.logical_not(away))
            def _():
                mine[...] = total[u * FB:(u + 1) * FB]

    pass_on(3)
    over_cores((1, 3))
    over_cores((0,))
    over_x(1)
    over_x(3)
    over_x(0)
    far_here(2)
    far_here(3)
    over_cores((2,))
    over_z(1)
    over_z(3)
    over_z(0)
    over_z(2)
    total = mine[...]
    for k in (0, 6, 1, 5, 2, 4, 3):
        arrived(r3.at[k], e3s.at[k], e3r.at[k])
        total += r3[k].astype(F32)
    s4[...] = total.T.astype(BF)
    post(s4, r4, e4s.at[0], e4r.at[0], owner)
    arrived(r4, e4s.at[0], e4r.at[0])
    out_ref[...] = r4[...].astype(F32)

    save_ctx.wait()
    for copy in sent:
        copy.wait_send()
    for n in range(GROUPS):
        for i in range(12):
            buf = (kb, vb)[i % 2].at[n, 0, 0]
            remote(buf, buf, bs.at[n, i], br.at[n, i], sibling).wait_send()
    for j in range(4):
        for u in range(2):
            away, copy = to_z(j, u)

            @pl.when(away)
            def _():
                copy.wait_send()


def on_device(enc_states, enc_len, queries, kv_weight, ctx_grad):
    any_spec = pl.BlockSpec(memory_space=pl.ANY)
    vmem = pltpu.VMEM
    dma = lambda *n: pltpu.SemaphoreType.DMA(n)
    context, enc_grad = pl.pallas_call(
        kernel,
        out_shape=(
            jax.ShapeDtypeStruct((DEC, COLS), BF),
            jax.ShapeDtypeStruct((TOK, FB), F32),
        ),
        in_specs=[any_spec, pl.BlockSpec(memory_space=pltpu.SMEM)] + [any_spec] * 3,
        out_specs=(any_spec, pl.BlockSpec(memory_space=pltpu.VMEM)),
        scratch_shapes=[
            vmem((4, TOK, ROWS), BF),
            vmem((ROWS, 2, COLS), BF),
            vmem((ROWS, 2 * COLS), BF),
            vmem((DEC, COLS), BF),
            vmem((DEC, COLS), BF),
            vmem((GROUPS, 4, 2, TOK, HEAD_DIM), F32),
            vmem((GROUPS, 4, 2, TOK, HEAD_DIM), BF),
            vmem((GROUPS, 2, TOK, HEAD_DIM), F32),
            vmem((GROUPS, 2, TOK, HEAD_DIM), BF),
            vmem((GROUPS, 2, TOK, HEAD_DIM), F32),
            vmem((GROUPS, 2, TOK, HEAD_DIM), BF),
            vmem((GROUPS, 2, 2, TOK, HEAD_DIM), F32),
            vmem((GROUPS, 2, 2, TOK, HEAD_DIM), BF),
            vmem((GROUPS, 4, 2, TOK, 2 * HEAD_DIM), BF),
            vmem((DEC, COLS), BF),
            vmem((4, ROWS, TOK), F32),
            vmem((4, HALF, TOK), BF),
            vmem((4, HALF, TOK), BF),
            vmem((4, 3, 2 * FB, TOK), BF),
            vmem((3, 4, 2 * FB, TOK), BF),
            vmem((4, 2, FB, TOK), BF),
            vmem((7, FB, TOK), BF),
            vmem((FB, TOK), F32),
            vmem((TOK, FB), BF),
            vmem((TOK, FB), BF),
            dma(4), dma(1), dma(1), dma(7), dma(7), dma(3, 4), dma(3, 4), dma(4), dma(4),
            dma(GROUPS, 12), dma(GROUPS, 12), dma(GROUPS, 4), dma(GROUPS, 4), dma(4, 4), dma(4, 4),
            dma(3, 4), dma(3, 4), dma(8), dma(7), dma(1), dma(1),
        ],
        compiler_params=pltpu.CompilerParams(
            collective_id=0, has_side_effects=True, vmem_limit_bytes=48 * 2**20
        ),
    )(
        enc_states[0],
        enc_len,
        queries[0, 0],
        kv_weight[0],
        ctx_grad[0, 0],
    )
    return (context[None, None], enc_grad[None])


def solution(mesh):
    return jax.shard_map(
        on_device,
        mesh=mesh,
        in_specs=(
            P("dp", None, ("pipe", "tensor")),
            P("dp"),
            P("pipe", "dp", None, "tensor"),
            P("pipe", "dp", None, "tensor"),
            P("pipe", "dp", None, "tensor"),
        ),
        out_specs=(P("pipe", "dp", None, "tensor"), P("dp", None, ("pipe", "tensor"))),
        check_vma=False,
    )
```
